256 devices in a mesh: run: 32 (over z, y), rep: 8 (over x, core).
Axes of the slice: x: 4, y: 4, z: 8, core: 2. Of those that a mesh axis runs over, the one named last changes fastest.
Arguments:
- edge_feats: bfloat16 [8, 65536, 1280], P('rep', 'run'), may hold values from -6 to 6
- edge_grads: bfloat16 [8, 65536, 640], P('rep', 'run'), may hold values from -0.059814453 to 0.059814453
- edge_system: int32 [8, 65536], P('rep', 'run'), may hold values from 0 to 5, as said below
- edge_count: int32 [8, 32], P('rep', 'run'), may hold values from 1025 to 2048
- coef: float32 [8, 6, 32], P('rep'), may hold values from 0.05 to 1
- weights: float32 [32, 1280, 640], P('rep', 'run'), may hold values from -0.15625 to 0.15625
- first_moment: float32 [32, 1280, 640], P('rep', 'run'), may hold values from -6 to 6
- second_moment: float32 [32, 1280, 640], P('rep', 'run'), may hold values from 1 to 10
Outputs:
- new_weights: float32 [32, 1280, 640], P('rep', 'run')
- new_first: float32 [32, 1280, 640], P('rep', 'run')
- new_second: float32 [32, 1280, 640], P('rep', 'run')
- merged_next: bfloat16 [8, 6, 1280, 640], P('rep', None, 'run')
The draws below stay inside these ranges and needn't reach their ends.
Inputs may be any that keep to these rules, and one draw needn't show every extreme that they name: `edge_system`: along each replica's rows the system never falls; every system number appears; the live rows of one device belong to one or two systems, two on some device in every draw.
All inputs are finite; a program needn't handle non-finite values.
Results may differ from the reference program's by a relative error of at most 0.001.
The reference program's roundings to bfloat16 on the way (of `rounded`) count: a program that leaves them out, or rounds other values in their place, can miss the bound.
Values may be sent and summed in bfloat16 or wider, within the bound.
No kernel may reach another device: no remote copies, remote signals or barrier semaphores. Data moves between devices by JAX's collectives and lax.ppermute only.
A program may use at most 128 MiB of HBM per device.

```python
import math
import jax
import jax.numpy as jnp
from jax import lax

DIN = 1280
DOUT = 640
EXPERTS = 32
NSYS = 6
ROWS = 2048
EDGES = 65536
N_RUN = 32
N_REP = 8


def draw_edge_system(key, part):

    def replica_ids(replica_key):
        key_block, key_offset = jax.random.split(replica_key)
        blocks = jnp.sort(jax.random.randint(key_block, (NSYS - 1,), 0, N_RUN - NSYS + 1))
        offsets = jnp.sort(jax.random.randint(key_offset, (NSYS - 1,), 1, ROWS // 2 + 1))
        bounds = (jnp.arange(1, NSYS) + blocks) * ROWS + offsets
        position = jnp.arange(N_RUN * ROWS)
        return jnp.sum((position[:, None] >= bounds[None, :]).astype(jnp.int32), axis=1).astype(jnp.int32)
    replica_keys = jax.random.split(key, N_REP)
    return jax.vmap(replica_ids)(replica_keys)


def place_ends(values, rng, smallest, top_value):
    dims = values.shape
    place = [jax.random.randint(jax.random.fold_in(rng, axis), (), 0, dims[axis]) for axis in range(len(dims))]
    values = values.at[tuple(place)].set(smallest)
    longest = dims.index(max(dims))
    place[longest] = (place[longest] + 1) % dims[longest]
    return values.at[tuple(place)].set(top_value)


def block_scale(stream_key, shape, shards, low, high):
    level, own = 1.0, jax.random.fold_in(stream_key, 6)
    for axis_at, shards_of in shards:
        draws = jnp.exp(jax.random.uniform(jax.random.fold_in(own, axis_at), (shards_of,), jnp.float32, low / len(shards), high / len(shards)))
        level = level * jnp.repeat(draws, shape[axis_at] // shards_of).reshape([-1 if axis == axis_at else 1 for axis in range(len(shape))])
    return level


def scatter_about(rng, extent, scale, reach, cuts=(), dtype=jnp.bfloat16):
    result = jax.random.normal(rng, extent, jnp.float32) * scale
    if len(cuts) > 0:
        result = block_scale(rng, extent, cuts, -0.22, 0.18) * result
    return jnp.clip(result, min=-reach, max=reach).astype(dtype)


def setup_inputs(seed: int = 0) -> dict:
    keys = jax.random.split(jax.random.key(seed), 9)
    edge_feats = scatter_about(keys[0], (N_REP, EDGES, DIN), 1.0, 6.0, ((0, 8), (1, 32)))
    edge_grads = scatter_about(keys[1], (N_REP, EDGES, DOUT), 0.01, 0.059814453, ((0, 8), (1, 32)))
    edge_system = draw_edge_system(jax.random.fold_in(keys[8], 71), 0)
    edge_count = place_ends(jax.random.randint(keys[3], (N_REP, N_RUN), ROWS // 2 + 1, ROWS + 1), jax.random.fold_in(keys[3], 1), ROWS // 2 + 1, ROWS).astype(jnp.int32)
    coef = jnp.clip(jnp.exp(math.log(1.0) - 2.9957323 * jax.random.uniform(keys[4], (N_REP, NSYS, EXPERTS), jnp.float32) ** block_scale(keys[4], (N_REP, NSYS, EXPERTS), ((0, 8),), -0.2, 0.2)), 0.05, 1.0)
    weights = scatter_about(keys[5], (EXPERTS, DIN, DOUT), DIN ** -0.5, 0.15625, ((0, 8), (1, 32)), jnp.float32)
    first_moment = scatter_about(keys[6], (EXPERTS, DIN, DOUT), 1.0, 6.0, ((0, 8), (1, 32)), jnp.float32)
    second_moment = jnp.clip(jnp.exp(math.log(10.0) - 2.3025851 * jax.random.uniform(keys[7], (EXPERTS, DIN, DOUT), jnp.float32) ** block_scale(keys[7], (EXPERTS, DIN, DOUT), ((0, 8), (1, 32)), -0.2, 0.2)), 1.0, 10.0)
    return {"edge_feats": edge_feats, "edge_grads": edge_grads, "edge_system": edge_system, "edge_count": edge_count, "coef": coef, "weights": weights, "first_moment": first_moment, "second_moment": second_moment}


def system_sums(feats, grads, system, counts):
    feat_blocks = feats.reshape(N_RUN, ROWS, DIN)
    grad_blocks = grads.reshape(N_RUN, ROWS, DOUT)
    sys_blocks = system.reshape(N_RUN, ROWS)

    def device_step(total, item):
        feat_rows, grad_rows, sys_rows, live_count = item
        live = jnp.arange(ROWS) < live_count
        first = sys_rows[0]
        last = lax.dynamic_index_in_dim(sys_rows, live_count - 1, 0, keepdims=False)
        left = feat_rows.astype(jnp.float32)

        def slot(offset):
            keep = live & (sys_rows == first + offset)
            right = jnp.where(keep[:, None], grad_rows.astype(jnp.float32), jnp.float32(0.0))
            return lax.dot_general(left, right, (((0,), (0,)), ((), ())), precision=lax.Precision.HIGHEST)
        lower = slot(0)
        upper = lax.cond(last > first, lambda: slot(1), lambda: jnp.zeros_like(lower))
        total = total.at[first].add(lower)
        total = total.at[jnp.minimum(first + 1, NSYS - 1)].add(upper)
        return (total, None)
    start = jnp.zeros((NSYS, DIN, DOUT), jnp.float32)
    total, _ = lax.scan(device_step, start, (feat_blocks, grad_blocks, sys_blocks, counts))
    return total

def reference(edge_feats, edge_grads, edge_system, edge_count, coef, weights, first_moment, second_moment):

    def replica_step(total, item):
        feats, grads, system, counts, group_coef = item
        sums = system_sums(feats, grads, system, counts)
        mixed = jnp.einsum('se,sio->eio', group_coef, sums, precision=lax.Precision.HIGHEST)
        return (total + mixed, None)
    start = jnp.zeros((EXPERTS, DIN, DOUT), jnp.float32)
    expert_grad, _ = lax.scan(replica_step, start, (edge_feats, edge_grads, edge_system, edge_count, coef))
    new_first = 0.9 * first_moment + 0.1 * expert_grad
    new_second = 0.999 * second_moment + 0.001 * expert_grad * expert_grad
    corr_first = 1.0 - 0.9 ** 10
    corr_second = 1.0 - 0.999 ** 10
    new_weights = weights - 0.01 * (new_first / corr_first) / (jnp.sqrt(new_second / corr_second) + 1e-08)
    rounded = lax.optimization_barrier(new_weights.astype(jnp.bfloat16))
    flat = rounded.astype(jnp.float32).reshape(EXPERTS, DIN * DOUT)
    merged = jnp.einsum('rse,ek->rsk', coef, flat, precision=lax.Precision.HIGHEST)
    merged_next = merged.reshape(N_REP, NSYS, DIN, DOUT).astype(jnp.bfloat16)
    return (new_weights, new_first, new_second, merged_next)
```

```python
import jax
import jax.numpy as jnp
from jax import lax
from jax.experimental import pallas as pl
from jax.experimental.pallas import tpu as pltpu
from jax.sharding import PartitionSpec as P

F32 = jnp.float32
BF16 = jnp.bfloat16
MIB = 1 << 20


def product_kernel(count_ref, system_ref, feats_ref, grads_ref, out_ref, low_acc, high_acc):
    step = pl.program_id(0)
    steps = pl.num_programs(0)
    rows = feats_ref.shape[0]
    owners, per_owner, _ = out_ref.shape
    half = per_owner // 2
    count = count_ref[0, 0]
    first = system_ref[0, 0]

    def halve(_, span):
        lo, hi = span
        mid = (lo + hi) // 2
        same = system_ref[0, jnp.minimum(mid, count - 1)] == first
        inside = lo < hi
        return (
            jnp.where(inside & same, mid + 1, lo),
            jnp.where(inside & jnp.logical_not(same), mid, hi),
        )

    split, _ = lax.fori_loop(0, 12, halve, (jnp.int32(0), count))
    has_upper = split < count
    base = step * rows
    row = base + lax.broadcasted_iota(jnp.int32, (rows, 1), 0)

    def product(begin, end):
        kept = jnp.where((row >= begin) & (row < end), grads_ref[...].astype(F32), 0.0)
        return lax.dot_general(
            feats_ref[...],
            kept.astype(BF16),
            (((0,), (0,)), ((), ())),
            preferred_element_type=F32,
        )

    @pl.when(step == 0)
    def _():
        low_acc[...] = product(0, split)

    @pl.when((step > 0) & (base < split))
    def _():
        low_acc[...] += product(0, split)

    @pl.when(has_upper & (step == 0))
    def _():
        high_acc[...] = jnp.zeros_like(high_acc)

    @pl.when(has_upper & (base + rows > split) & (base < count))
    def _():
        high_acc[...] += product(split, count)

    @pl.when((step == steps - 1) & has_upper)
    def _():
        for owner in range(owners):
            low = low_acc[owner * half : (owner + 1) * half, :]
            high = high_acc[owner * half : (owner + 1) * half, :]
            out_ref[owner] = jnp.concatenate([low, high], axis=0).astype(BF16)

    @pl.when((step == steps - 1) & jnp.logical_not(has_upper))
    def _():
        for owner in range(owners):
            low = low_acc[owner * half : (owner + 1) * half, :]
            out_ref[owner] = jnp.concatenate([low, jnp.zeros_like(low)], axis=0).astype(BF16)


def products(count, system, feats, grads, owners):
    rows, din = feats.shape
    dout = grads.shape[1]
    block = 512
    per_owner = 2 * din // owners
    return pl.pallas_call(
        product_kernel,
        grid=(rows // block,),
        in_specs=[
            pl.BlockSpec(memory_space=pltpu.SMEM),
            pl.BlockSpec(memory_space=pltpu.SMEM),
            pl.BlockSpec((block, din), lambda k: (k, 0)),
            pl.BlockSpec((block, dout), lambda k: (k, 0)),
        ],
        out_specs=pl.BlockSpec((owners, per_owner, dout), lambda k: (0, 0, 0)),
        out_shape=jax.ShapeDtypeStruct((owners, per_owner, dout), BF16),
        scratch_shapes=[pltpu.VMEM((din, dout), F32), pltpu.VMEM((din, dout), F32)],
        compiler_params=pltpu.CompilerParams(vmem_limit_bytes=48 * MIB),
        cost_estimate=pl.CostEstimate(
            flops=2 * rows * din * dout,
            bytes_accessed=2 * rows * (din + dout) + 4 * din * dout,
            transcendentals=0,
        ),
        name="products",
    )(count, system, feats, grads)


def collect_kernel(first_ref, parts_ref, out_ref, total):
    step = pl.program_id(0)
    here = parts_ref.shape[0]
    nsys, half, _ = total.shape

    @pl.when(step == 0)
    def _():
        total[...] = jnp.zeros_like(total)

    for source in range(here):
        low = first_ref[step * here + source]
        high = jnp.minimum(low + 1, nsys - 1)
        part = parts_ref[source].astype(F32)
        total[low] += part[:half]
        total[high] += part[half:]

    @pl.when(step == pl.num_programs(0) - 1)
    def _():
        out_ref[...] = total[...].astype(BF16)


def collect(firsts, parts, nsys):
    sources, both, dout = parts.shape
    half = both // 2
    block = 8
    return pl.pallas_call(
        collect_kernel,
        grid=(sources // block,),
        in_specs=[
            pl.BlockSpec(memory_space=pltpu.SMEM),
            pl.BlockSpec((block, both, dout), lambda k: (k, 0, 0)),
        ],
        out_specs=pl.BlockSpec((nsys, half, dout), lambda k: (0, 0, 0)),
        out_shape=jax.ShapeDtypeStruct((nsys, half, dout), BF16),
        scratch_shapes=[pltpu.VMEM((nsys, half, dout), F32)],
        compiler_params=pltpu.CompilerParams(vmem_limit_bytes=32 * MIB),
        cost_estimate=pl.CostEstimate(
            flops=2 * sources * both * dout,
            bytes_accessed=2 * sources * both * dout,
            transcendentals=0,
        ),
        name="collect",
    )(firsts, parts)


def update_kernel(own_ref, mix_ref, merge_ref, *refs):
    sums = refs[:8]
    weights_ref, first_ref, second_ref = refs[8:11]
    out_weights, out_first, out_second, out_merged = refs[11:15]
    all_weights, all_first, all_second = refs[15:18]
    experts, rows, lanes = weights_ref.shape
    nsys = out_merged.shape[0]
    mine = out_weights.shape[0]
    corr_first = 1.0 - 0.9**10
    corr_second = 1.0 - 0.999**10
    group = 8
    system_sums = jnp.concatenate([ref[...].astype(F32) for ref in sums], axis=0)
    merged = []
    for g in range(rows // group):
        at = slice(g * group, (g + 1) * group)
        right = system_sums[:, at, :].reshape(-1, lanes).astype(BF16)
        both = jnp.dot(mix_ref[...], right, preferred_element_type=F32)
        n = experts * group
        grad = (both[:n] + both[n:]).reshape(experts, group, lanes)
        new_first = 0.9 * first_ref[:, at, :] + 0.1 * grad
        new_second = 0.999 * second_ref[:, at, :] + 0.001 * grad * grad
        new_weights = weights_ref[:, at, :] - 0.01 * (new_first / corr_first) / (
            jnp.sqrt(new_second / corr_second) + 1e-08
        )
        all_weights[:, at, :] = new_weights
        all_first[:, at, :] = new_first
        all_second[:, at, :] = new_second
        rounded = new_weights.reshape(n, lanes).astype(BF16)
        both = jnp.dot(merge_ref[...], rounded, preferred_element_type=F32)
        m = nsys * group
        merged.append((both[:m] + both[m:]).reshape(nsys, group, lanes))
    out_merged[...] = jnp.concatenate(merged, axis=1).astype(BF16)
    own = own_ref[0]
    out_weights[...] = all_weights[pl.ds(own, mine)]
    out_first[...] = all_first[pl.ds(own, mine)]
    out_second[...] = all_second[pl.ds(own, mine)]


def update(own, mix, merge, sums, weights, first_moment, second_moment, mine):
    experts, rows, dout = weights.shape
    nsys = sums[0].shape[0]
    lanes = 128
    whole = lambda k: (0, 0)
    column = lambda k: (0, 0, k)
    state = pl.BlockSpec((experts, rows, lanes), column)
    out_state = pl.BlockSpec((mine, rows, lanes), column)
    return pl.pallas_call(
        update_kernel,
        grid=(dout // lanes,),
        in_specs=[
            pl.BlockSpec(memory_space=pltpu.SMEM),
            pl.BlockSpec(mix.shape, whole),
            pl.BlockSpec(merge.shape, whole),
        ]
        + [pl.BlockSpec((nsys, rows, lanes), column)] * 8
        + [state] * 3,
        out_specs=[out_state] * 3 + [pl.BlockSpec((nsys, rows, lanes), column)],
        out_shape=[jax.ShapeDtypeStruct((mine, rows, dout), F32)] * 3
        + [jax.ShapeDtypeStruct((nsys, rows, dout), BF16)],
        scratch_shapes=[pltpu.VMEM((experts, rows, lanes), F32)] * 3,
        compiler_params=pltpu.CompilerParams(vmem_limit_bytes=48 * MIB),
        name="update",
    )(own, mix, merge, *sums, weights, first_moment, second_moment)


def in_two_parts(matrix):
    high = lax.reduce_precision(matrix, 8, 7)
    return jnp.concatenate([high, matrix - high], axis=0).astype(BF16)


def on_device(
    edge_feats, edge_grads, edge_system, edge_count, coef, weights, first_moment, second_moment
):
    owners = lax.axis_size("run")
    reps = lax.axis_size("rep")
    nsys = coef.shape[1]
    mine = weights.shape[0]
    rep = lax.axis_index("rep")
    firsts = lax.all_gather(edge_system[0, :1], "run", axis=0, tiled=True)
    coefs = lax.all_gather(coef, "rep", axis=0, tiled=True)
    all_weights = lax.all_gather(weights, "rep", axis=0, tiled=True)
    all_first = lax.all_gather(first_moment, "rep", axis=0, tiled=True)
    all_second = lax.all_gather(second_moment, "rep", axis=0, tiled=True)

    chips = reps // 2
    offsets = [(dx, other) for other in (0, 1) for dx in (0, -1, 1, 2)]
    chip, core = rep // 2, rep % 2
    order = jnp.stack(
        [(chip + dx + chips) % chips * 2 + (core + other) % 2 for dx, other in offsets]
    )
    eye = jnp.eye(8, dtype=F32)
    chosen = (order[:, None] == jnp.arange(reps))[:, :, None, None]
    ordered = jnp.sum(jnp.where(chosen, coefs[None], 0.0), axis=1).reshape(reps * nsys, -1)
    mix = in_two_parts(jnp.kron(ordered.T, eye))
    merge = in_two_parts(jnp.kron(coef[0], eye))

    parts = products(edge_count, edge_system, edge_feats[0], edge_grads[0], owners)
    received = lax.all_to_all(parts, "run", 0, 0, tiled=True)
    sums = collect(firsts, received, nsys)

    def from_chip(dx):
        pairs = [((x + dx) % chips * 2 + c, x * 2 + c) for x in range(chips) for c in range(2)]
        return lax.ppermute(sums, "rep", pairs)

    near = [sums] + [from_chip(dx) for dx in (-1, 1, 2)]
    swap = [(i, i ^ 1) for i in range(reps)]
    far = [lax.ppermute(part, "rep", swap) for part in near]
    new_weights, new_first, new_second, merged = update(
        (rep * mine).reshape(1), mix, merge, near + far, all_weights, all_first, all_second, mine
    )
    return (new_weights, new_first, new_second, merged[None])


def solution(mesh):
    placed = (
        P("rep", "run", None),
        P("rep", "run", None),
        P("rep", "run"),
        P("rep", "run"),
        P("rep", None, None),
        P("rep", "run", None),
        P("rep", "run", None),
        P("rep", "run", None),
    )
    return jax.shard_map(
        on_device,
        mesh=mesh,
        in_specs=placed,
        out_specs=(
            P("rep", "run", None),
            P("rep", "run", None),
            P("rep", "run", None),
            P("rep", None, "run", None),
        ),
        check_vma=False,
    )
```

```python
import jax
import jax.numpy as jnp
from jax import lax
from jax.experimental import pallas as pl
from jax.experimental.pallas import tpu as pltpu
from jax.sharding import PartitionSpec as P

F32 = jnp.float32
BF16 = jnp.bfloat16
I16 = jnp.int16
MIB = 1 << 20
LANES = 128
NOTE = 16


def exponent(largest):
    return jnp.ceil(jnp.log2(jnp.maximum(largest, 1e-30) * (1.0 / 32700.0)))


def coded(values):
    return jnp.round(values).astype(jnp.int32).astype(I16)


def plain(codes):
    return codes.astype(jnp.int32).astype(F32)


def product_kernel(count_ref, system_ref, feats_ref, grads_ref, out_ref, low_acc, high_acc):
    step = pl.program_id(0)
    steps = pl.num_programs(0)
    rows = feats_ref.shape[0]
    owners = out_ref.shape[0]
    half = low_acc.shape[0] // owners
    blocks = low_acc.shape[1] // LANES
    count = count_ref[0, 0]
    first = system_ref[0, 0]

    def halve(_, span):
        lo, hi = span
        mid = (lo + hi) // 2
        same = system_ref[0, jnp.minimum(mid, count - 1)] == first
        inside = lo < hi
        return (
            jnp.where(inside & same, mid + 1, lo),
            jnp.where(inside & jnp.logical_not(same), mid, hi),
        )

    split, _ = lax.fori_loop(0, 12, halve, (jnp.int32(0), count))
    has_upper = split < count
    base = step * rows
    row = base + lax.broadcasted_iota(jnp.int32, (rows, 1), 0)

    def product(begin, end):
        kept = jnp.where((row >= begin) & (row < end), grads_ref[...].astype(F32), 0.0)
        return lax.dot_general(
            feats_ref[...],
            kept.astype(BF16),
            (((0,), (0,)), ((), ())),
            preferred_element_type=F32,
        )

    @pl.when(step == 0)
    def _():
        low_acc[...] = product(0, split)

    @pl.when((step > 0) & (base < split))
    def _():
        low_acc[...] += product(0, split)

    @pl.when(has_upper & (step == 0))
    def _():
        high_acc[...] = jnp.zeros_like(high_acc)

    @pl.when(has_upper & (base + rows > split) & (base < count))
    def _():
        high_acc[...] += product(split, count)

    def hand_out(low_e, high_e):
        row = lax.broadcasted_iota(jnp.int32, (NOTE, LANES), 0)
        note = jnp.where(row == 0, first.astype(F32), jnp.where(row == 1, low_e, high_e))
        note = coded(note)
        low_by = jnp.exp2(-low_e)
        high_by = None if isinstance(high_e, float) else jnp.exp2(-high_e)
        for owner in range(owners):
            at = slice(owner * half, (owner + 1) * half)
            for block in range(blocks):
                lanes = slice(block * LANES, (block + 1) * LANES)
                low = low_acc[at, lanes] * low_by
                high = jnp.zeros_like(low) if high_by is None else high_acc[at, lanes] * high_by
                to = slice(block * 2 * half, (block + 1) * 2 * half)
                out_ref[owner, to, :] = coded(jnp.concatenate([low, high], axis=0))
            out_ref[owner, blocks * 2 * half :, :] = note

    def largest(ref):
        return jnp.max(jnp.abs(ref[...]), axis=(0, 1), keepdims=True)

    @pl.when((step == steps - 1) & has_upper)
    def _():
        hand_out(exponent(largest(low_acc)), exponent(largest(high_acc)))

    @pl.when((step == steps - 1) & jnp.logical_not(has_upper))
    def _():
        hand_out(exponent(largest(low_acc)), 0.0)


def products(count, system, feats, grads, owners):
    rows, din = feats.shape
    dout = grads.shape[1]
    block = 512
    per_owner = 2 * din // owners * (dout // LANES) + NOTE
    return pl.pallas_call(
        product_kernel,
        grid=(rows // block,),
        in_specs=[
            pl.BlockSpec(memory_space=pltpu.SMEM),
            pl.BlockSpec(memory_space=pltpu.SMEM),
            pl.BlockSpec((block, din), lambda k: (k, 0)),
            pl.BlockSpec((block, dout), lambda k: (k, 0)),
        ],
        out_specs=pl.BlockSpec((owners, per_owner, LANES), lambda k: (0, 0, 0)),
        out_shape=jax.ShapeDtypeStruct((owners, per_owner, LANES), I16),
        scratch_shapes=[pltpu.VMEM((din, dout), F32), pltpu.VMEM((din, dout), F32)],
        compiler_params=pltpu.CompilerParams(vmem_limit_bytes=62 * MIB),
        cost_estimate=pl.CostEstimate(
            flops=2 * rows * din * dout,
            bytes_accessed=2 * rows * (din + dout) + 4 * din * dout,
            transcendentals=0,
        ),
        name="products",
    )(count, system, feats, grads)


def collect_kernel(parts_ref, out_ref, total):
    step = pl.program_id(0)
    nsys, half, dout = total.shape
    blocks = dout // LANES

    @pl.when(step == 0)
    def _():
        total[...] = jnp.zeros_like(total)

    for source in range(parts_ref.shape[0]):
        note = plain(parts_ref[source, blocks * 2 * half :, :])
        low = jnp.max(note[0:1]).astype(jnp.int32)
        high = jnp.minimum(low + 1, nsys - 1)
        low_by, high_by = jnp.exp2(note[1:2]), jnp.exp2(note[2:3])
        for block in range(blocks):
            lanes = slice(block * LANES, (block + 1) * LANES)
            part = plain(parts_ref[source, block * 2 * half : (block + 1) * 2 * half, :])
            total[low, :, lanes] += part[:half] * low_by
            total[high, :, lanes] += part[half:] * high_by

    @pl.when(step == pl.num_programs(0) - 1)
    def _():
        row = lax.broadcasted_iota(jnp.int32, (NOTE, dout), 0)
        note = jnp.zeros((NOTE, dout), F32)
        scaled = []
        for system in range(nsys):
            values = total[system]
            e = exponent(jnp.max(jnp.abs(values), axis=(0, 1), keepdims=True))
            note = jnp.where(row == system, e, note)
            scaled.append(values * jnp.exp2(-e))
        out_ref[...] = coded(jnp.concatenate(scaled + [note], axis=0))


def collect(parts, nsys, half, dout):
    sources = parts.shape[0]
    block = 8
    out = (nsys * half + NOTE, dout)
    return pl.pallas_call(
        collect_kernel,
        grid=(sources // block,),
        in_specs=[pl.BlockSpec((block,) + parts.shape[1:], lambda k: (k, 0, 0))],
        out_specs=pl.BlockSpec(out, lambda k: (0, 0)),
        out_shape=jax.ShapeDtypeStruct(out, I16),
        scratch_shapes=[pltpu.VMEM((nsys, half, dout), F32)],
        compiler_params=pltpu.CompilerParams(vmem_limit_bytes=12 * MIB),
        cost_estimate=pl.CostEstimate(
            flops=2 * parts.size, bytes_accessed=2 * parts.size, transcendentals=0
        ),
        name="collect",
    )(parts)


def update_kernel(mix_ref, merge_ref, *refs):
    sums = refs[:8]
    states = refs[8:16]
    out_weights, out_first, out_second, out_merged = refs[16:20]
    system_sums, merged = refs[20:22]
    step = pl.program_id(0)
    mine, group, lanes = out_weights.shape
    nsys, rows, _ = merged.shape
    n = group * mine * len(states)
    m = group * nsys
    corr_first = 1.0 - 0.9**10
    corr_second = 1.0 - 0.999**10

    @pl.when(step == 0)
    def _():
        for rep, ref in enumerate(sums):
            note = plain(ref[nsys * rows :, :])
            values = plain(ref[: nsys * rows, :])
            for system in range(nsys):
                by = jnp.exp2(note[system : system + 1])
                system_sums[rep * nsys + system] = values[system * rows : (system + 1) * rows] * by

    def of_experts(kind):
        return jnp.concatenate([ref[kind * mine : (kind + 1) * mine] for ref in states], axis=0)

    at = pl.ds(pl.multiple_of(step * group, group), group)
    right = system_sums[:, at, :].reshape(-1, lanes)
    near = right.astype(BF16)
    rest = (right - near.astype(F32)).astype(BF16)
    both = jnp.dot(mix_ref[...], near, preferred_element_type=F32)
    more = jnp.dot(mix_ref[:n, :], rest, preferred_element_type=F32)
    grad = (both[:n] + (both[n:] + more)).reshape(-1, group, lanes)
    new_first = 0.9 * of_experts(1) + 0.1 * grad
    new_second = 0.999 * of_experts(2) + 0.001 * grad * grad
    new_weights = of_experts(0) - 0.01 * (new_first / corr_first) / (
        jnp.sqrt(new_second / corr_second) + 1e-08
    )
    out_weights[...] = new_weights[:mine]
    out_first[...] = new_first[:mine]
    out_second[...] = new_second[:mine]
    rounded = new_weights.reshape(n, lanes).astype(BF16)
    both = jnp.dot(merge_ref[...], rounded, preferred_element_type=F32)
    merged[:, at, :] = (both[:m] + both[m:]).reshape(nsys, group, lanes)

    @pl.when(step == pl.num_programs(0) - 1)
    def _():
        out_merged[...] = merged[...].astype(BF16)


def update(mix, merge, sums, states, nsys):
    mine, rows, dout = states[0].shape
    mine = mine // 3
    group = 8
    whole = lambda g: (0, 0)
    some = lambda g: (0, g, 0)
    return pl.pallas_call(
        update_kernel,
        grid=(rows // group,),
        in_specs=[pl.BlockSpec(a.shape, whole) for a in [mix, merge] + sums]
        + [pl.BlockSpec((3 * mine, group, dout), some)] * 8,
        out_specs=[pl.BlockSpec((mine, group, dout), some)] * 3
        + [pl.BlockSpec((nsys, rows, dout), lambda g: (0, 0, 0))],
        out_shape=[jax.ShapeDtypeStruct((mine, rows, dout), F32)] * 3
        + [jax.ShapeDtypeStruct((nsys, rows, dout), BF16)],
        scratch_shapes=[
            pltpu.VMEM((8 * nsys, rows, dout), F32),
            pltpu.VMEM((nsys, rows, dout), F32),
        ],
        compiler_params=pltpu.CompilerParams(vmem_limit_bytes=32 * MIB),
        name="update",
    )(mix, merge, *sums, *states)


def in_two_parts(matrix):
    high = lax.reduce_precision(matrix, 8, 7)
    return jnp.concatenate([high, matrix - high], axis=0).astype(BF16)


def everywhere(value, axis, moves):
    return [lax.ppermute(value, axis, pairs) for pairs in moves]


def on_device(
    edge_feats, edge_grads, edge_system, edge_count, coef, weights, first_moment, second_moment
):
    owners = lax.axis_size("run")
    reps = lax.axis_size("rep")
    nsys = coef.shape[1]

    chips = reps // 2
    along_x = [
        [((x + dx) % chips * 2 + c, x * 2 + c) for x in range(chips) for c in range(2)]
        for dx in range(1, chips)
    ]
    swap = [(i, i ^ 1) for i in range(reps)]

    def all_reps(value):
        near = [value] + everywhere(value, "rep", along_x)
        return near + [lax.ppermute(part, "rep", swap) for part in near]

    coefs = jnp.stack(all_reps(coef[0]))
    states = all_reps(jnp.concatenate([weights, first_moment, second_moment], axis=0))

    rep = lax.axis_index("rep")
    chip, core = rep // 2, rep % 2
    order = jnp.stack(
        [(chip + dx) % chips * 2 + (core + other) % 2 for other in (0, 1) for dx in range(chips)]
    )
    chosen = (order[:, None] == jnp.arange(reps))[:, :, None]
    by_owner = coefs.reshape(reps * nsys, 1, reps, -1)
    ordered = jnp.sum(jnp.where(chosen, by_owner, 0.0), axis=2).reshape(reps * nsys, -1)
    eye = jnp.eye(8, dtype=F32)
    mix = in_two_parts(jnp.kron(ordered.T, eye))
    merge = in_two_parts(jnp.kron(ordered[:nsys], eye))

    parts = products(edge_count, edge_system, edge_feats[0], edge_grads[0], owners)
    received = lax.all_to_all(parts, "run", 0, 0, tiled=True)
    sums = all_reps(collect(received, nsys, weights.shape[1], weights.shape[2]))
    new_weights, new_first, new_second, merged = update(mix, merge, sums, states, nsys)
    return (new_weights, new_first, new_second, merged[None])


def solution(mesh):
    placed = (
        P("rep", "run", None),
        P("rep", "run", None),
        P("rep", "run"),
        P("rep", "run"),
        P("rep", None, None),
        P("rep", "run", None),
        P("rep", "run", None),
        P("rep", "run", None),
    )
    return jax.shard_map(
        on_device,
        mesh=mesh,
        in_specs=placed,
        out_specs=(
            P("rep", "run", None),
            P("rep", "run", None),
            P("rep", "run", None),
            P("rep", None, "run", None),
        ),
        check_vma=False,
    )
```

```python
import jax
import jax.numpy as jnp
from jax import lax
from jax.experimental import pallas as pl
from jax.experimental.pallas import tpu as pltpu
from jax.sharding import PartitionSpec as P

F32 = jnp.float32
BF16 = jnp.bfloat16
I16 = jnp.int16
MIB = 1 << 20
LANES = 128
NOTE = 16


def exponent(largest):
    return jnp.ceil(jnp.log2(jnp.maximum(largest, 1e-30) * (1.0 / 32700.0)))


def coded(values):
    return jnp.round(values).astype(jnp.int32).astype(I16)


def plain(codes):
    return codes.astype(jnp.int32).astype(F32)


def product_kernel(count_ref, system_ref, feats_ref, grads_ref, out_ref, low_acc, high_acc):
    step = pl.program_id(0)
    steps = pl.num_programs(0)
    rows = feats_ref.shape[0]
    owners = out_ref.shape[0]
    half = low_acc.shape[0] // owners
    blocks = low_acc.shape[1] // LANES
    count = count_ref[0, 0]
    first = system_ref[0, 0]

    def halve(_, span):
        lo, hi = span
        mid = (lo + hi) // 2
        same = system_ref[0, jnp.minimum(mid, count - 1)] == first
        inside = lo < hi
        return (
            jnp.where(inside & same, mid + 1, lo),
            jnp.where(inside & jnp.logical_not(same), mid, hi),
        )

    split, _ = lax.fori_loop(0, 12, halve, (jnp.int32(0), count))
    has_upper = split < count
    base = step * rows
    row = base + lax.broadcasted_iota(jnp.int32, (rows, 1), 0)

    def product(begin, end):
        kept = jnp.where((row >= begin) & (row < end), grads_ref[...].astype(F32), 0.0)
        return lax.dot_general(
            feats_ref[...],
            kept.astype(BF16),
            (((0,), (0,)), ((), ())),
            preferred_element_type=F32,
        )

    @pl.when(step == 0)
    def _():
        low_acc[...] = product(0, split)

    @pl.when((step > 0) & (base < split))
    def _():
        low_acc[...] += product(0, split)

    @pl.when(has_upper & (step == 0))
    def _():
        high_acc[...] = jnp.zeros_like(high_acc)

    @pl.when(has_upper & (base + rows > split) & (base < count))
    def _():
        high_acc[...] += product(split, count)

    def hand_out(low_e, high_e):
        row = lax.broadcasted_iota(jnp.int32, (NOTE, LANES), 0)
        note = jnp.where(row == 0, first.astype(F32), jnp.where(row == 1, low_e, high_e))
        note = coded(note)
        low_by = jnp.exp2(-low_e)
        high_by = None if isinstance(high_e, float) else jnp.exp2(-high_e)
        for owner in range(owners):
            at = slice(owner * half, (owner + 1) * half)
            for block in range(blocks):
                lanes = slice(block * LANES, (block + 1) * LANES)
                low = low_acc[at, lanes] * low_by
                high = jnp.zeros_like(low) if high_by is None else high_acc[at, lanes] * high_by
                to = slice(block * 2 * half, (block + 1) * 2 * half)
                out_ref[owner, to, :] = coded(jnp.concatenate([low, high], axis=0))
            out_ref[owner, blocks * 2 * half :, :] = note

    def largest(ref):
        return jnp.max(jnp.abs(ref[...]), axis=(0, 1), keepdims=True)

    @pl.when((step == steps - 1) & has_upper)
    def _():
        hand_out(exponent(largest(low_acc)), exponent(largest(high_acc)))

    @pl.when((step == steps - 1) & jnp.logical_not(has_upper))
    def _():
        hand_out(exponent(largest(low_acc)), 0.0)


def products(count, system, feats, grads, owners):
    rows, din = feats.shape
    dout = grads.shape[1]
    block = 512
    per_owner = 2 * din // owners * (dout // LANES) + NOTE
    return pl.pallas_call(
        product_kernel,
        grid=(rows // block,),
        in_specs=[
            pl.BlockSpec(memory_space=pltpu.SMEM),
            pl.BlockSpec(memory_space=pltpu.SMEM),
            pl.BlockSpec((block, din), lambda k: (k, 0)),
            pl.BlockSpec((block, dout), lambda k: (k, 0)),
        ],
        out_specs=pl.BlockSpec((owners, per_owner, LANES), lambda k: (0, 0, 0)),
        out_shape=jax.ShapeDtypeStruct((owners, per_owner, LANES), I16),
        scratch_shapes=[pltpu.VMEM((din, dout), F32), pltpu.VMEM((din, dout), F32)],
        compiler_params=pltpu.CompilerParams(vmem_limit_bytes=62 * MIB),
        cost_estimate=pl.CostEstimate(
            flops=2 * rows * din * dout,
            bytes_accessed=2 * rows * (din + dout) + 4 * din * dout,
            transcendentals=0,
        ),
        name="products",
    )(count, system, feats, grads)


def collect_kernel(parts_ref, out_ref, total):
    step = pl.program_id(0)
    nsys, half, dout = total.shape
    blocks = dout // LANES

    @pl.when(step == 0)
    def _():
        total[...] = jnp.zeros_like(total)

    for source in range(parts_ref.shape[0]):
        note = plain(parts_ref[source, blocks * 2 * half :, :])
        low = jnp.max(note[0:1]).astype(jnp.int32)
        high = jnp.minimum(low + 1, nsys - 1)
        low_by, high_by = jnp.exp2(note[1:2]), jnp.exp2(note[2:3])
        for block in range(blocks):
            lanes = slice(block * LANES, (block + 1) * LANES)
            part = plain(parts_ref[source, block * 2 * half : (block + 1) * 2 * half, :])
            total[low, :, lanes] += part[:half] * low_by
            total[high, :, lanes] += part[half:] * high_by

    @pl.when(step == pl.num_programs(0) - 1)
    def _():
        row = lax.broadcasted_iota(jnp.int32, (NOTE, dout), 0)
        note = jnp.zeros((NOTE, dout), F32)
        scaled = []
        for system in range(nsys):
            values = total[system]
            e = exponent(jnp.max(jnp.abs(values), axis=(0, 1), keepdims=True))
            note = jnp.where(row == system, e, note)
            scaled.append(values * jnp.exp2(-e))
        out_ref[...] = coded(jnp.concatenate(scaled + [note], axis=0))


def collect(parts, nsys, half, dout):
    sources = parts.shape[0]
    block = 8
    out = (nsys * half + NOTE, dout)
    return pl.pallas_call(
        collect_kernel,
        grid=(sources // block,),
        in_specs=[pl.BlockSpec((block,) + parts.shape[1:], lambda k: (k, 0, 0))],
        out_specs=pl.BlockSpec(out, lambda k: (0, 0)),
        out_shape=jax.ShapeDtypeStruct(out, I16),
        scratch_shapes=[pltpu.VMEM((nsys, half, dout), F32)],
        compiler_params=pltpu.CompilerParams(vmem_limit_bytes=12 * MIB),
        cost_estimate=pl.CostEstimate(
            flops=2 * parts.size, bytes_accessed=2 * parts.size, transcendentals=0
        ),
        name="collect",
    )(parts)


def update_kernel(mix_ref, merge_ref, *refs):
    sums = refs[:8]
    states = refs[8:16]
    out_weights, out_first, out_second, out_merged = refs[16:20]
    system_sums, merged = refs[20:22]
    step = pl.program_id(0)
    mine, group, lanes = out_weights.shape
    nsys, rows, _ = merged.shape
    n = group * mine * len(states)
    m = group * nsys
    corr_first = 1.0 - 0.9**10
    corr_second = 1.0 - 0.999**10

    @pl.when(step == 0)
    def _():
        for rep, ref in enumerate(sums):
            note = plain(ref[nsys * rows :, :])
            values = plain(ref[: nsys * rows, :])
            for system in range(nsys):
                by = jnp.exp2(note[system : system + 1])
                system_sums[rep * nsys + system] = values[system * rows : (system + 1) * rows] * by

    def of_experts(kind):
        return jnp.concatenate([ref[kind * mine : (kind + 1) * mine] for ref in states], axis=0)

    at = pl.ds(pl.multiple_of(step * group, group), group)
    right = system_sums[:, at, :].reshape(-1, lanes)
    near = right.astype(BF16)
    rest = (right - near.astype(F32)).astype(BF16)
    both = jnp.dot(mix_ref[...], near, preferred_element_type=F32)
    more = jnp.dot(mix_ref[:n, :], rest, preferred_element_type=F32)
    grad = (both[:n] + (both[n:] + more)).reshape(-1, group, lanes)
    new_first = 0.9 * of_experts(1) + 0.1 * grad
    new_second = 0.999 * of_experts(2) + 0.001 * grad * grad
    new_weights = of_experts(0) - 0.01 * (new_first / corr_first) / (
        jnp.sqrt(new_second / corr_second) + 1e-08
    )
    out_weights[...] = new_weights[:mine]
    out_first[...] = new_first[:mine]
    out_second[...] = new_second[:mine]
    rounded = new_weights.reshape(n, lanes).astype(BF16)
    both = jnp.dot(merge_ref[...], rounded, preferred_element_type=F32)
    merged[:, at, :] = (both[:m] + both[m:]).reshape(nsys, group, lanes)

    @pl.when(step == pl.num_programs(0) - 1)
    def _():
        out_merged[...] = merged[...].astype(BF16)


def update(mix, merge, sums, states, nsys):
    mine, rows, dout = states[0].shape
    mine = mine // 3
    group = 8
    whole = lambda g: (0, 0)
    some = lambda g: (0, g, 0)
    return pl.pallas_call(
        update_kernel,
        grid=(rows // group,),
        in_specs=[pl.BlockSpec(a.shape, whole) for a in [mix, merge] + sums]
        + [pl.BlockSpec((3 * mine, group, dout), some)] * 8,
        out_specs=[pl.BlockSpec((mine, group, dout), some)] * 3
        + [pl.BlockSpec((nsys, rows, dout), lambda g: (0, 0, 0))],
        out_shape=[jax.ShapeDtypeStruct((mine, rows, dout), F32)] * 3
        + [jax.ShapeDtypeStruct((nsys, rows, dout), BF16)],
        scratch_shapes=[
            pltpu.VMEM((8 * nsys, rows, dout), F32),
            pltpu.VMEM((nsys, rows, dout), F32),
        ],
        compiler_params=pltpu.CompilerParams(vmem_limit_bytes=32 * MIB),
        name="update",
    )(mix, merge, *sums, *states)


def prepare_kernel(rep_ref, *refs):
    coefs, (mix_ref, merge_ref) = refs[:-2], refs[-2:]
    reps, chips = len(coefs), len(coefs) // 2
    padded, experts = coefs[0].shape
    rows = mix_ref.shape[0] // 2
    columns = mix_ref.shape[1]
    out_rows = merge_ref.shape[0] // 2
    nsys = out_rows // 8
    mine = experts // reps
    chip, core = rep_ref[0] // 2, rep_ref[0] % 2

    def count(shape, axis):
        return lax.broadcasted_iota(jnp.int32, shape, axis)

    expert = count((rows, experts), 0) >> 3
    block = expert // mine
    owner = ((chip + block % chips) % chips) * 2 + (core + block // chips) % 2
    at_expert = owner * mine + expert % mine == count((rows, experts), 1)
    at_expert = at_expert.astype(F32).astype(BF16)
    row = count((padded * reps, columns), 0)
    place = row % padded
    at_system = (count((padded * reps, columns), 1) >> 3) == nsys * (row // padded) + place
    at_system = (at_system & (place < nsys)).astype(F32).astype(BF16)
    at_out = (count((out_rows, padded), 0) >> 3) == count((out_rows, padded), 1)
    at_out = at_out.astype(F32).astype(BF16)
    same_mix = (count((rows, columns), 0) & 7) == (count((rows, columns), 1) & 7)
    same_merge = (count((out_rows, rows), 0) & 7) == (count((out_rows, rows), 1) & 7)
    values = jnp.concatenate([ref[...] for ref in coefs], axis=0)
    near = values.astype(BF16)
    rest = (values - near.astype(F32)).astype(BF16)
    transposed = (((1,), (1,)), ((), ()))
    for k, part in enumerate((near, rest)):
        wide = lax.dot_general(at_expert, part, transposed, preferred_element_type=F32)
        wide = jnp.dot(wide.astype(BF16), at_system, preferred_element_type=F32)
        mix_ref[k * rows : (k + 1) * rows, :] = jnp.where(same_mix, wide, 0.0).astype(BF16)
        own = jnp.dot(at_out, part[:padded], preferred_element_type=F32)
        own = lax.dot_general(own.astype(BF16), at_expert, transposed, preferred_element_type=F32)
        merge_ref[k * out_rows : (k + 1) * out_rows, :] = jnp.where(same_merge, own, 0.0).astype(BF16)


def prepare(rep, coefs, nsys):
    reps, experts = len(coefs), coefs[0].shape[1]
    vmem = pl.BlockSpec(memory_space=pltpu.VMEM)
    return pl.pallas_call(
        prepare_kernel,
        in_specs=[pl.BlockSpec(memory_space=pltpu.SMEM)] + [vmem] * reps,
        out_specs=[vmem, vmem],
        out_shape=[
            jax.ShapeDtypeStruct((2 * 8 * experts, 8 * reps * nsys), BF16),
            jax.ShapeDtypeStruct((2 * 8 * nsys, 8 * experts), BF16),
        ],
        compiler_params=pltpu.CompilerParams(vmem_limit_bytes=12 * MIB),
        name="prepare",
    )(rep, *coefs)


def everywhere(value, axis, moves):
    return [lax.ppermute(value, axis, pairs) for pairs in moves]


def on_device(
    edge_feats, edge_grads, edge_system, edge_count, coef, weights, first_moment, second_moment
):
    owners = lax.axis_size("run")
    reps = lax.axis_size("rep")
    nsys = coef.shape[1]

    chips = reps // 2
    along_x = [
        [((x + dx) % chips * 2 + c, x * 2 + c) for x in range(chips) for c in range(2)]
        for dx in range(1, chips)
    ]
    swap = [(i, i ^ 1) for i in range(reps)]

    def all_reps(value):
        near = [value] + everywhere(value, "rep", along_x)
        return near + [lax.ppermute(part, "rep", swap) for part in near]

    coefs = all_reps(jnp.pad(coef[0], ((0, -nsys % 8), (0, 0))))
    mix, merge = prepare(lax.axis_index("rep").reshape(1), coefs, nsys)
    mix, merge, *state_parts = lax.optimization_barrier(
        (mix, merge, weights, first_moment, second_moment)
    )
    states = all_reps(jnp.concatenate(state_parts, axis=0))

    parts = products(edge_count, edge_system, edge_feats[0], edge_grads[0], owners)
    received = lax.all_to_all(parts, "run", 0, 0, tiled=True)
    sums = all_reps(collect(received, nsys, weights.shape[1], weights.shape[2]))
    new_weights, new_first, new_second, merged = update(mix, merge, sums, states, nsys)
    return (new_weights, new_first, new_second, merged[None])


def solution(mesh):
    placed = (
        P("rep", "run", None),
        P("rep", "run", None),
        P("rep", "run"),
        P("rep", "run"),
        P("rep", None, None),
        P("rep", "run", None),
        P("rep", "run", None),
        P("rep", "run", None),
    )
    return jax.shard_map(
        on_device,
        mesh=mesh,
        in_specs=placed,
        out_specs=(
            P("rep", "run", None),
            P("rep", "run", None),
            P("rep", "run", None),
            P("rep", None, "run", None),
        ),
        check_vma=False,
    )
```

```python
import jax
import jax.numpy as jnp
from jax import lax
from jax.experimental import pallas as pl
from jax.experimental.pallas import tpu as pltpu
from jax.sharding import PartitionSpec as P

F32 = jnp.float32
BF16 = jnp.bfloat16
I16 = jnp.int16
MIB = 1 << 20
LANES = 128
NOTE = 16


def exponent(largest):
    return jnp.ceil(jnp.log2(jnp.maximum(largest, 1e-30) * (1.0 / 32700.0)))


def coded(values):
    return jnp.round(values).astype(jnp.int32).astype(I16)


def plain(codes):
    return codes.astype(jnp.int32).astype(F32)


def product_kernel(count_ref, system_ref, feats_ref, grads_ref, out_ref, low_acc, high_acc):
    step = pl.program_id(0)
    steps = pl.num_programs(0)
    rows = feats_ref.shape[0]
    owners = out_ref.shape[0]
    half = low_acc.shape[0] // owners
    blocks = low_acc.shape[1] // LANES
    count = count_ref[0, 0]
    first = system_ref[0, 0]

    def halve(_, span):
        lo, hi = span
        mid = (lo + hi) // 2
        same = system_ref[0, jnp.minimum(mid, count - 1)] == first
        inside = lo < hi
        return (
            jnp.where(inside & same, mid + 1, lo),
            jnp.where(inside & jnp.logical_not(same), mid, hi),
        )

    split, _ = lax.fori_loop(0, 12, halve, (jnp.int32(0), count))
    has_upper = split < count
    base = step * rows
    row = base + lax.broadcasted_iota(jnp.int32, (rows, 1), 0)

    def product(begin, end):
        kept = jnp.where((row >= begin) & (row < end), grads_ref[...].astype(F32), 0.0)
        return lax.dot_general(
            feats_ref[...],
            kept.astype(BF16),
            (((0,), (0,)), ((), ())),
            preferred_element_type=F32,
        )

    @pl.when(step == 0)
    def _():
        low_acc[...] = product(0, split)

    @pl.when((step > 0) & (base < split))
    def _():
        low_acc[...] += product(0, split)

    @pl.when(has_upper & (step == 0))
    def _():
        high_acc[...] = jnp.zeros_like(high_acc)

    @pl.when(has_upper & (base + rows > split) & (base < count))
    def _():
        high_acc[...] += product(split, count)

    def hand_out(low_e, high_e):
        row = lax.broadcasted_iota(jnp.int32, (NOTE, LANES), 0)
        note = jnp.where(row == 0, first.astype(F32), jnp.where(row == 1, low_e, high_e))
        note = coded(note)
        low_by = jnp.exp2(-low_e)
        high_by = None if isinstance(high_e, float) else jnp.exp2(-high_e)
        for owner in range(owners):
            at = slice(owner * half, (owner + 1) * half)
            for block in range(blocks):
                lanes = slice(block * LANES, (block + 1) * LANES)
                low = low_acc[at, lanes] * low_by
                high = jnp.zeros_like(low) if high_by is None else high_acc[at, lanes] * high_by
                to = slice(block * 2 * half, (block + 1) * 2 * half)
                out_ref[owner, to, :] = coded(jnp.concatenate([low, high], axis=0))
            out_ref[owner, blocks * 2 * half :, :] = note

    def largest(ref):
        return jnp.max(jnp.abs(ref[...]), axis=(0, 1), keepdims=True)

    @pl.when((step == steps - 1) & has_upper)
    def _():
        hand_out(exponent(largest(low_acc)), exponent(largest(high_acc)))

    @pl.when((step == steps - 1) & jnp.logical_not(has_upper))
    def _():
        hand_out(exponent(largest(low_acc)), 0.0)


def products(count, system, feats, grads, owners):
    rows, din = feats.shape
    dout = grads.shape[1]
    block = 512
    per_owner = 2 * din // owners * (dout // LANES) + NOTE
    return pl.pallas_call(
        product_kernel,
        grid=(rows // block,),
        in_specs=[
            pl.BlockSpec(memory_space=pltpu.SMEM),
            pl.BlockSpec(memory_space=pltpu.SMEM),
            pl.BlockSpec((block, din), lambda k: (k, 0)),
            pl.BlockSpec((block, dout), lambda k: (k, 0)),
        ],
        out_specs=pl.BlockSpec((owners, per_owner, LANES), lambda k: (0, 0, 0)),
        out_shape=jax.ShapeDtypeStruct((owners, per_owner, LANES), I16),
        scratch_shapes=[pltpu.VMEM((din, dout), F32), pltpu.VMEM((din, dout), F32)],
        compiler_params=pltpu.CompilerParams(vmem_limit_bytes=62 * MIB),
        cost_estimate=pl.CostEstimate(
            flops=2 * rows * din * dout,
            bytes_accessed=2 * rows * (din + dout) + 4 * din * dout,
            transcendentals=0,
        ),
        name="products",
    )(count, system, feats, grads)


def collect_kernel(parts_ref, out_ref, total):
    step = pl.program_id(0)
    nsys, half, dout = total.shape
    blocks = dout // LANES

    @pl.when(step == 0)
    def _():
        total[...] = jnp.zeros_like(total)

    for source in range(parts_ref.shape[0]):
        note = plain(parts_ref[source, blocks * 2 * half :, :])
        low = jnp.max(note[0:1]).astype(jnp.int32)
        high = jnp.minimum(low + 1, nsys - 1)
        low_by, high_by = jnp.exp2(note[1:2]), jnp.exp2(note[2:3])
        for block in range(blocks):
            lanes = slice(block * LANES, (block + 1) * LANES)
            part = plain(parts_ref[source, block * 2 * half : (block + 1) * 2 * half, :])
            total[low, :, lanes] += part[:half] * low_by
            total[high, :, lanes] += part[half:] * high_by

    @pl.when(step == pl.num_programs(0) - 1)
    def _():
        row = lax.broadcasted_iota(jnp.int32, (NOTE, LANES), 0)
        note = jnp.zeros((NOTE, LANES), F32)
        scaled = []
        for system in range(nsys):
            values = total[system]
            e = exponent(jnp.max(jnp.abs(values), axis=(0, 1), keepdims=True))
            note = jnp.where(row == system, e, note)
            scaled.append(values * jnp.exp2(-e))
        rows = nsys * half
        for block in range(blocks):
            lanes = slice(block * LANES, (block + 1) * LANES)
            values = jnp.concatenate([part[:, lanes] for part in scaled], axis=0)
            out_ref[block * rows : (block + 1) * rows, :] = coded(values)
        out_ref[blocks * rows :, :] = coded(note)


def collect(parts, nsys, half, dout):
    sources = parts.shape[0]
    block = 8
    out = (nsys * half * (dout // LANES) + NOTE, LANES)
    return pl.pallas_call(
        collect_kernel,
        grid=(sources // block,),
        in_specs=[pl.BlockSpec((block,) + parts.shape[1:], lambda k: (k, 0, 0))],
        out_specs=pl.BlockSpec(out, lambda k: (0, 0)),
        out_shape=jax.ShapeDtypeStruct(out, I16),
        scratch_shapes=[pltpu.VMEM((nsys, half, dout), F32)],
        compiler_params=pltpu.CompilerParams(vmem_limit_bytes=12 * MIB),
        cost_estimate=pl.CostEstimate(
            flops=2 * parts.size, bytes_accessed=2 * parts.size, transcendentals=0
        ),
        name="collect",
    )(parts)


def update_kernel(mix_ref, merge_ref, *refs):
    sums = refs[:8]
    states = refs[8:16]
    out_weights, out_first, out_second, out_merged = refs[16:20]
    system_sums, merged = refs[20:22]
    step = pl.program_id(0)
    mine, group, lanes = out_weights.shape
    nsys, rows, _ = merged.shape
    n = group * mine * len(states)
    m = group * nsys
    corr_first = 1.0 - 0.9**10
    corr_second = 1.0 - 0.999**10

    @pl.when(step == 0)
    def _():
        for rep, ref in enumerate(sums):
            per_block = nsys * rows
            by = jnp.exp2(plain(ref[lanes // LANES * per_block :, :]))
            for block in range(lanes // LANES):
                to = slice(block * LANES, (block + 1) * LANES)
                values = plain(ref[block * per_block : (block + 1) * per_block, :])
                for system in range(nsys):
                    system_sums[rep * nsys + system, :, to] = (
                        values[system * rows : (system + 1) * rows] * by[system : system + 1]
                    )

    def of_experts(kind):
        return jnp.concatenate([ref[kind * mine : (kind + 1) * mine] for ref in states], axis=0)

    at = pl.ds(pl.multiple_of(step * group, group), group)
    right = system_sums[:, at, :].reshape(-1, lanes)
    near = right.astype(BF16)
    rest = (right - near.astype(F32)).astype(BF16)
    both = jnp.dot(mix_ref[...], near, preferred_element_type=F32)
    more = jnp.dot(mix_ref[:n, :], rest, preferred_element_type=F32)
    grad = (both[:n] + (both[n:] + more)).reshape(-1, group, lanes)
    new_first = 0.9 * of_experts(1) + 0.1 * grad
    new_second = 0.999 * of_experts(2) + 0.001 * grad * grad
    scaled = new_second * (1.0 / corr_second)
    below = scaled * lax.rsqrt(scaled) + 1e-08
    inverse = pl.reciprocal(below, approx=True)
    inverse = inverse * (2.0 - below * inverse)
    new_weights = of_experts(0) - new_first * (0.01 / corr_first) * inverse
    out_weights[...] = new_weights[:mine]
    out_first[...] = new_first[:mine]
    out_second[...] = new_second[:mine]
    rounded = new_weights.reshape(n, lanes).astype(BF16)
    both = jnp.dot(merge_ref[...], rounded, preferred_element_type=F32)
    merged[:, at, :] = (both[:m] + both[m:]).reshape(nsys, group, lanes)

    @pl.when(step == pl.num_programs(0) - 1)
    def _():
        out_merged[...] = merged[...].astype(BF16)


def update(mix, merge, sums, states, nsys):
    mine, rows, dout = states[0].shape
    mine = mine // 3
    group = 8
    whole = lambda g: (0, 0)
    some = lambda g: (0, g, 0)
    return pl.pallas_call(
        update_kernel,
        grid=(rows // group,),
        in_specs=[pl.BlockSpec(a.shape, whole) for a in [mix, merge] + sums]
        + [pl.BlockSpec((3 * mine, group, dout), some)] * 8,
        out_specs=[pl.BlockSpec((mine, group, dout), some)] * 3
        + [pl.BlockSpec((nsys, rows, dout), lambda g: (0, 0, 0))],
        out_shape=[jax.ShapeDtypeStruct((mine, rows, dout), F32)] * 3
        + [jax.ShapeDtypeStruct((nsys, rows, dout), BF16)],
        scratch_shapes=[
            pltpu.VMEM((8 * nsys, rows, dout), F32),
            pltpu.VMEM((nsys, rows, dout), F32),
        ],
        compiler_params=pltpu.CompilerParams(vmem_limit_bytes=32 * MIB),
        name="update",
    )(mix, merge, *sums, *states)


def prepare_kernel(rep_ref, *refs):
    coefs, (mix_ref, merge_ref) = refs[:-2], refs[-2:]
    reps, chips = len(coefs), len(coefs) // 2
    padded, experts = coefs[0].shape
    rows = mix_ref.shape[0] // 2
    columns = mix_ref.shape[1]
    out_rows = merge_ref.shape[0] // 2
    nsys = out_rows // 8
    mine = experts // reps
    chip, core = rep_ref[0] // 2, rep_ref[0] % 2

    def count(shape, axis):
        return lax.broadcasted_iota(jnp.int32, shape, axis)

    expert = count((rows, experts), 0) >> 3
    block = expert // mine
    owner = ((chip + block % chips) % chips) * 2 + (core + block // chips) % 2
    at_expert = owner * mine + expert % mine == count((rows, experts), 1)
    at_expert = at_expert.astype(F32).astype(BF16)
    row = count((padded * reps, columns), 0)
    place = row % padded
    at_system = (count((padded * reps, columns), 1) >> 3) == nsys * (row // padded) + place
    at_system = (at_system & (place < nsys)).astype(F32).astype(BF16)
    at_out = (count((out_rows, padded), 0) >> 3) == count((out_rows, padded), 1)
    at_out = at_out.astype(F32).astype(BF16)
    same_mix = (count((rows, columns), 0) & 7) == (count((rows, columns), 1) & 7)
    same_merge = (count((out_rows, rows), 0) & 7) == (count((out_rows, rows), 1) & 7)
    values = jnp.concatenate([ref[...] for ref in coefs], axis=0)
    near = values.astype(BF16)
    rest = (values - near.astype(F32)).astype(BF16)
    transposed = (((1,), (1,)), ((), ()))
    for k, part in enumerate((near, rest)):
        wide = lax.dot_general(at_expert, part, transposed, preferred_element_type=F32)
        wide = jnp.dot(wide.astype(BF16), at_system, preferred_element_type=F32)
        mix_ref[k * rows : (k + 1) * rows, :] = jnp.where(same_mix, wide, 0.0).astype(BF16)
        own = jnp.dot(at_out, part[:padded], preferred_element_type=F32)
        own = lax.dot_general(own.astype(BF16), at_expert, transposed, preferred_element_type=F32)
        merge_ref[k * out_rows : (k + 1) * out_rows, :] = jnp.where(same_merge, own, 0.0).astype(BF16)


def prepare(rep, coefs, nsys):
    reps, experts = len(coefs), coefs[0].shape[1]
    vmem = pl.BlockSpec(memory_space=pltpu.VMEM)
    return pl.pallas_call(
        prepare_kernel,
        in_specs=[pl.BlockSpec(memory_space=pltpu.SMEM)] + [vmem] * reps,
        out_specs=[vmem, vmem],
        out_shape=[
            jax.ShapeDtypeStruct((2 * 8 * experts, 8 * reps * nsys), BF16),
            jax.ShapeDtypeStruct((2 * 8 * nsys, 8 * experts), BF16),
        ],
        compiler_params=pltpu.CompilerParams(vmem_limit_bytes=12 * MIB),
        name="prepare",
    )(rep, *coefs)


def everywhere(value, axis, moves):
    return [lax.ppermute(value, axis, pairs) for pairs in moves]


def on_device(
    edge_feats, edge_grads, edge_system, edge_count, coef, weights, first_moment, second_moment
):
    owners = lax.axis_size("run")
    reps = lax.axis_size("rep")
    nsys = coef.shape[1]

    chips = reps // 2
    along_x = [
        [((x + dx) % chips * 2 + c, x * 2 + c) for x in range(chips) for c in range(2)]
        for dx in range(1, chips)
    ]
    swap = [(i, i ^ 1) for i in range(reps)]

    def all_reps(value):
        near = [value] + everywhere(value, "rep", along_x)
        return near + [lax.ppermute(part, "rep", swap) for part in near]

    coefs = all_reps(jnp.pad(coef[0], ((0, -nsys % 8), (0, 0))))
    mix, merge = prepare(lax.axis_index("rep").reshape(1), coefs, nsys)
    mix, merge, *state_parts = lax.optimization_barrier(
        (mix, merge, weights, first_moment, second_moment)
    )
    states = all_reps(jnp.concatenate(state_parts, axis=0))

    parts = products(edge_count, edge_system, edge_feats[0], edge_grads[0], owners)
    received = lax.all_to_all(parts, "run", 0, 0, tiled=True)
    sums = all_reps(collect(received, nsys, weights.shape[1], weights.shape[2]))
    new_weights, new_first, new_second, merged = update(mix, merge, sums, states, nsys)
    return (new_weights, new_first, new_second, merged[None])


def solution(mesh):
    placed = (
        P("rep", "run", None),
        P("rep", "run", None),
        P("rep", "run"),
        P("rep", "run"),
        P("rep", None, None),
        P("rep", "run", None),
        P("rep", "run", None),
        P("rep", "run", None),
    )
    return jax.shard_map(
        on_device,
        mesh=mesh,
        in_specs=placed,
        out_specs=(
            P("rep", "run", None),
            P("rep", "run", None),
            P("rep", "run", None),
            P("rep", None, "run", None),
        ),
        check_vma=False,
    )
```

```python
import jax
import jax.numpy as jnp
from jax import lax
from jax.experimental import pallas as pl
from jax.experimental.pallas import tpu as pltpu
from jax.sharding import PartitionSpec as P

F32 = jnp.float32
BF16 = jnp.bfloat16
I16 = jnp.int16
MIB = 1 << 20
LANES = 128
NOTE = 16


def exponent(largest):
    return jnp.ceil(jnp.log2(jnp.maximum(largest, 1e-30) * (1.0 / 32700.0)))


def coded(values):
    return jnp.round(values).astype(jnp.int32).astype(I16)


def plain(codes):
    return codes.astype(jnp.int32).astype(F32)


def product_kernel(count_ref, system_ref, feats_ref, grads_ref, out_ref, low_acc, high_acc):
    step = pl.program_id(0)
    steps = pl.num_programs(0)
    rows = feats_ref.shape[0]
    owners = out_ref.shape[0]
    half = low_acc.shape[0] // owners
    blocks = low_acc.shape[1] // LANES
    count = count_ref[0, 0]
    first = system_ref[0, 0]

    def halve(_, span):
        lo, hi = span
        mid = (lo + hi) // 2
        same = system_ref[0, jnp.minimum(mid, count - 1)] == first
        inside = lo < hi
        return (
            jnp.where(inside & same, mid + 1, lo),
            jnp.where(inside & jnp.logical_not(same), mid, hi),
        )

    split, _ = lax.fori_loop(0, 12, halve, (jnp.int32(0), count))
    has_upper = split < count
    base = step * rows
    row = base + lax.broadcasted_iota(jnp.int32, (rows, 1), 0)

    def product(begin, end):
        kept = jnp.where((row >= begin) & (row < end), grads_ref[...].astype(F32), 0.0)
        return lax.dot_general(
            feats_ref[...],
            kept.astype(BF16),
            (((0,), (0,)), ((), ())),
            preferred_element_type=F32,
        )

    @pl.when(step == 0)
    def _():
        low_acc[...] = product(0, split)

    @pl.when((step > 0) & (base < split))
    def _():
        low_acc[...] += product(0, split)

    @pl.when(has_upper & (step == 0))
    def _():
        high_acc[...] = jnp.zeros_like(high_acc)

    @pl.when(has_upper & (base + rows > split) & (base < count))
    def _():
        high_acc[...] += product(split, count)

    def hand_out(low_e, high_e):
        row = lax.broadcasted_iota(jnp.int32, (NOTE, LANES), 0)
        note = jnp.where(row == 0, first.astype(F32), jnp.where(row == 1, low_e, high_e))
        note = coded(note)
        low_by = jnp.exp2(-low_e)
        high_by = None if isinstance(high_e, float) else jnp.exp2(-high_e)
        for owner in range(owners):
            at = slice(owner * half, (owner + 1) * half)
            for block in range(blocks):
                lanes = slice(block * LANES, (block + 1) * LANES)
                low = low_acc[at, lanes] * low_by
                high = jnp.zeros_like(low) if high_by is None else high_acc[at, lanes] * high_by
                to = slice(block * 2 * half, (block + 1) * 2 * half)
                out_ref[owner, to, :] = coded(jnp.concatenate([low, high], axis=0))
            out_ref[owner, blocks * 2 * half :, :] = note

    def largest(ref):
        return jnp.max(jnp.abs(ref[...]), axis=(0, 1), keepdims=True)

    @pl.when((step == steps - 1) & has_upper)
    def _():
        hand_out(exponent(largest(low_acc)), exponent(largest(high_acc)))

    @pl.when((step == steps - 1) & jnp.logical_not(has_upper))
    def _():
        hand_out(exponent(largest(low_acc)), 0.0)


def products(count, system, feats, grads, owners):
    rows, din = feats.shape
    dout = grads.shape[1]
    block = 512
    per_owner = 2 * din // owners * (dout // LANES) + NOTE
    return pl.pallas_call(
        product_kernel,
        grid=(rows // block,),
        in_specs=[
            pl.BlockSpec(memory_space=pltpu.SMEM),
            pl.BlockSpec(memory_space=pltpu.SMEM),
            pl.BlockSpec((block, din), lambda k: (k, 0)),
            pl.BlockSpec((block, dout), lambda k: (k, 0)),
        ],
        out_specs=pl.BlockSpec((owners, per_owner, LANES), lambda k: (0, 0, 0)),
        out_shape=jax.ShapeDtypeStruct((owners, per_owner, LANES), I16),
        scratch_shapes=[pltpu.VMEM((din, dout), F32), pltpu.VMEM((din, dout), F32)],
        compiler_params=pltpu.CompilerParams(vmem_limit_bytes=62 * MIB),
        cost_estimate=pl.CostEstimate(
            flops=2 * rows * din * dout,
            bytes_accessed=2 * rows * (din + dout) + 4 * din * dout,
            transcendentals=0,
        ),
        name="products",
    )(count, system, feats, grads)


def collect_kernel(parts_ref, out_ref, total):
    step = pl.program_id(0)
    nsys, half, dout = total.shape
    blocks = dout // LANES

    @pl.when(step == 0)
    def _():
        total[...] = jnp.zeros_like(total)

    for source in range(parts_ref.shape[0]):
        note = plain(parts_ref[source, blocks * 2 * half :, :])
        low = jnp.max(note[0:1]).astype(jnp.int32)
        high = jnp.minimum(low + 1, nsys - 1)
        low_by, high_by = jnp.exp2(note[1:2]), jnp.exp2(note[2:3])
        for block in range(blocks):
            lanes = slice(block * LANES, (block + 1) * LANES)
            part = plain(parts_ref[source, block * 2 * half : (block + 1) * 2 * half, :])
            total[low, :, lanes] += part[:half] * low_by
            total[high, :, lanes] += part[half:] * high_by

    @pl.when(step == pl.num_programs(0) - 1)
    def _():
        row = lax.broadcasted_iota(jnp.int32, (NOTE, LANES), 0)
        note = jnp.zeros((NOTE, LANES), F32)
        scaled = []
        for system in range(nsys):
            values = total[system]
            e = exponent(jnp.max(jnp.abs(values), axis=(0, 1), keepdims=True))
            note = jnp.where(row == system, e, note)
            scaled.append(values * jnp.exp2(-e))
        rows = nsys * half
        for block in range(blocks):
            lanes = slice(block * LANES, (block + 1) * LANES)
            values = jnp.concatenate([part[:, lanes] for part in scaled], axis=0)
            out_ref[block * rows : (block + 1) * rows, :] = coded(values)
        out_ref[blocks * rows :, :] = coded(note)


def collect(parts, nsys, half, dout):
    sources = parts.shape[0]
    block = 8
    out = (nsys * half * (dout // LANES) + NOTE, LANES)
    return pl.pallas_call(
        collect_kernel,
        grid=(sources // block,),
        in_specs=[pl.BlockSpec((block,) + parts.shape[1:], lambda k: (k, 0, 0))],
        out_specs=pl.BlockSpec(out, lambda k: (0, 0)),
        out_shape=jax.ShapeDtypeStruct(out, I16),
        scratch_shapes=[pltpu.VMEM((nsys, half, dout), F32)],
        compiler_params=pltpu.CompilerParams(vmem_limit_bytes=12 * MIB),
        cost_estimate=pl.CostEstimate(
            flops=2 * parts.size, bytes_accessed=2 * parts.size, transcendentals=0
        ),
        name="collect",
    )(parts)


def hold_kernel(*refs):
    states, held_ref, sems = refs[:-2], refs[-2], refs[-1]
    copies = [
        pltpu.make_async_copy(ref, held_ref.at[k], sems.at[k]) for k, ref in enumerate(states)
    ]
    for copy in copies:
        copy.start()
    for copy in copies:
        copy.wait()


def hold(states):
    shape = (len(states),) + states[0].shape
    return pl.pallas_call(
        hold_kernel,
        in_specs=[pl.BlockSpec(memory_space=pl.ANY)] * len(states),
        out_specs=pl.BlockSpec(memory_space=pltpu.VMEM),
        out_shape=pltpu.VMEM(shape, F32),
        scratch_shapes=[pltpu.SemaphoreType.DMA((len(states),))],
        compiler_params=pltpu.CompilerParams(vmem_limit_bytes=4 * MIB),
        name="hold",
    )(*states)


def update_kernel(mix_ref, merge_ref, *refs):
    sums, states = refs[:8], refs[8]
    out_weights, out_first, out_second, out_merged, system_sums, merged = refs[9:]
    step = pl.program_id(0)
    mine, group, lanes = out_weights.shape
    nsys, rows, _ = merged.shape
    reps = states.shape[0]
    n = group * mine * reps
    at = pl.ds(pl.multiple_of(step * group, group), group)
    m = group * nsys
    corr_first = 1.0 - 0.9**10
    corr_second = 1.0 - 0.999**10

    @pl.when(step == 0)
    def _():
        for rep, ref in enumerate(sums):
            per_block = nsys * rows
            by = jnp.exp2(plain(ref[lanes // LANES * per_block :, :]))
            for block in range(lanes // LANES):
                to = slice(block * LANES, (block + 1) * LANES)
                values = plain(ref[block * per_block : (block + 1) * per_block, :])
                for system in range(nsys):
                    system_sums[rep * nsys + system, :, to] = (
                        values[system * rows : (system + 1) * rows] * by[system : system + 1]
                    )

    def of_experts(kind):
        return states[:, kind * mine : (kind + 1) * mine, at, :].reshape(-1, group, lanes)

    right = system_sums[:, at, :].reshape(-1, lanes)
    near = right.astype(BF16)
    rest = (right - near.astype(F32)).astype(BF16)
    both = jnp.dot(mix_ref[...], near, preferred_element_type=F32)
    more = jnp.dot(mix_ref[:n, :], rest, preferred_element_type=F32)
    grad = (both[:n] + (both[n:] + more)).reshape(-1, group, lanes)
    new_first = 0.9 * of_experts(1) + 0.1 * grad
    new_second = 0.999 * of_experts(2) + 0.001 * grad * grad
    scaled = new_second * (1.0 / corr_second)
    below = scaled * lax.rsqrt(scaled) + 1e-08
    inverse = pl.reciprocal(below, approx=True)
    inverse = inverse * (2.0 - below * inverse)
    new_weights = of_experts(0) - new_first * (0.01 / corr_first) * inverse
    out_weights[...] = new_weights[:mine]
    out_first[...] = new_first[:mine]
    out_second[...] = new_second[:mine]
    rounded = new_weights.reshape(n, lanes).astype(BF16)
    both = jnp.dot(merge_ref[...], rounded, preferred_element_type=F32)
    merged[:, at, :] = (both[:m] + both[m:]).reshape(nsys, group, lanes)

    @pl.when(step == pl.num_programs(0) - 1)
    def _():
        out_merged[...] = merged[...].astype(BF16)


def update(mix, merge, sums, states, nsys):
    reps, mine, rows, dout = states.shape
    mine = mine // 3
    group = 8
    whole = lambda g: (0, 0)
    some = lambda g: (0, g, 0)
    return pl.pallas_call(
        update_kernel,
        grid=(rows // group,),
        in_specs=[pl.BlockSpec(a.shape, whole) for a in [mix, merge] + sums]
        + [pl.BlockSpec(memory_space=pltpu.VMEM)],
        out_specs=[pl.BlockSpec((mine, group, dout), some)] * 3
        + [pl.BlockSpec((nsys, rows, dout), lambda g: (0, 0, 0))],
        out_shape=[jax.ShapeDtypeStruct((mine, rows, dout), F32)] * 3
        + [jax.ShapeDtypeStruct((nsys, rows, dout), BF16)],
        scratch_shapes=[
            pltpu.VMEM((8 * nsys, rows, dout), F32),
            pltpu.VMEM((nsys, rows, dout), F32),
        ],
        compiler_params=pltpu.CompilerParams(vmem_limit_bytes=32 * MIB),
        name="update",
    )(mix, merge, *sums, states)


def prepare_kernel(rep_ref, *refs):
    coefs, (mix_ref, merge_ref) = refs[:-2], refs[-2:]
    reps, chips = len(coefs), len(coefs) // 2
    padded, experts = coefs[0].shape
    rows = mix_ref.shape[0] // 2
    columns = mix_ref.shape[1]
    out_rows = merge_ref.shape[0] // 2
    nsys = out_rows // 8
    mine = experts // reps
    chip, core = rep_ref[0] // 2, rep_ref[0] % 2

    def count(shape, axis):
        return lax.broadcasted_iota(jnp.int32, shape, axis)

    expert = count((rows, experts), 0) >> 3
    block = expert // mine
    owner = ((chip + block % chips) % chips) * 2 + (core + block // chips) % 2
    at_expert = owner * mine + expert % mine == count((rows, experts), 1)
    at_expert = at_expert.astype(F32).astype(BF16)
    row = count((padded * reps, columns), 0)
    place = row % padded
    at_system = (count((padded * reps, columns), 1) >> 3) == nsys * (row // padded) + place
    at_system = (at_system & (place < nsys)).astype(F32).astype(BF16)
    at_out = (count((out_rows, padded), 0) >> 3) == count((out_rows, padded), 1)
    at_out = at_out.astype(F32).astype(BF16)
    same_mix = (count((rows, columns), 0) & 7) == (count((rows, columns), 1) & 7)
    same_merge = (count((out_rows, rows), 0) & 7) == (count((out_rows, rows), 1) & 7)
    values = jnp.concatenate([ref[...] for ref in coefs], axis=0)
    near = values.astype(BF16)
    rest = (values - near.astype(F32)).astype(BF16)
    transposed = (((1,), (1,)), ((), ()))
    for k, part in enumerate((near, rest)):
        wide = lax.dot_general(at_expert, part, transposed, preferred_element_type=F32)
        wide = jnp.dot(wide.astype(BF16), at_system, preferred_element_type=F32)
        mix_ref[k * rows : (k + 1) * rows, :] = jnp.where(same_mix, wide, 0.0).astype(BF16)
        own = jnp.dot(at_out, part[:padded], preferred_element_type=F32)
        own = lax.dot_general(own.astype(BF16), at_expert, transposed, preferred_element_type=F32)
        merge_ref[k * out_rows : (k + 1) * out_rows, :] = jnp.where(same_merge, own, 0.0).astype(BF16)


def prepare(rep, coefs, nsys):
    reps, experts = len(coefs), coefs[0].shape[1]
    vmem = pl.BlockSpec(memory_space=pltpu.VMEM)
    return pl.pallas_call(
        prepare_kernel,
        in_specs=[pl.BlockSpec(memory_space=pltpu.SMEM)] + [vmem] * reps,
        out_specs=[vmem, vmem],
        out_shape=[
            jax.ShapeDtypeStruct((2 * 8 * experts, 8 * reps * nsys), BF16),
            jax.ShapeDtypeStruct((2 * 8 * nsys, 8 * experts), BF16),
        ],
        compiler_params=pltpu.CompilerParams(vmem_limit_bytes=12 * MIB),
        name="prepare",
    )(rep, *coefs)


def everywhere(value, axis, moves):
    return [lax.ppermute(value, axis, pairs) for pairs in moves]


def on_device(
    edge_feats, edge_grads, edge_system, edge_count, coef, weights, first_moment, second_moment
):
    owners = lax.axis_size("run")
    reps = lax.axis_size("rep")
    nsys = coef.shape[1]

    chips = reps // 2
    along_x = [
        [((x + dx) % chips * 2 + c, x * 2 + c) for x in range(chips) for c in range(2)]
        for dx in range(1, chips)
    ]
    swap = [(i, i ^ 1) for i in range(reps)]

    def all_reps(value):
        near = [value] + everywhere(value, "rep", along_x)
        return near + [lax.ppermute(part, "rep", swap) for part in near]

    coefs = all_reps(jnp.pad(coef[0], ((0, -nsys % 8), (0, 0))))
    mix, merge = prepare(lax.axis_index("rep").reshape(1), coefs, nsys)
    mix, merge, *state_parts = lax.optimization_barrier(
        (mix, merge, weights, first_moment, second_moment)
    )
    states = all_reps(jnp.concatenate(state_parts, axis=0))

    parts = products(edge_count, edge_system, edge_feats[0], edge_grads[0], owners)
    received = lax.all_to_all(parts, "run", 0, 0, tiled=True)
    sums = collect(received, nsys, weights.shape[1], weights.shape[2])
    near = [sums] + everywhere(sums, "rep", along_x)
    *states, after = lax.optimization_barrier((*states, sums))
    states, after = lax.optimization_barrier((hold(states), after))
    sums = near + [lax.ppermute(part, "rep", swap) for part in [after] + near[1:]]
    new_weights, new_first, new_second, merged = update(mix, merge, sums, states, nsys)
    return (new_weights, new_first, new_second, merged[None])


def solution(mesh):
    placed = (
        P("rep", "run", None),
        P("rep", "run", None),
        P("rep", "run"),
        P("rep", "run"),
        P("rep", None, None),
        P("rep", "run", None),
        P("rep", "run", None),
        P("rep", "run", None),
    )
    return jax.shard_map(
        on_device,
        mesh=mesh,
        in_specs=placed,
        out_specs=(
            P("rep", "run", None),
            P("rep", "run", None),
            P("rep", "run", None),
            P("rep", None, "run", None),
        ),
        check_vma=False,
    )
```

```python
import jax
import jax.numpy as jnp
from jax import lax
from jax.experimental import pallas as pl
from jax.experimental.pallas import tpu as pltpu
from jax.sharding import PartitionSpec as P

F32 = jnp.float32
BF16 = jnp.bfloat16
I16 = jnp.int16
MIB = 1 << 20
LANES = 128
NOTE = 16


def exponent(largest):
    return jnp.ceil(jnp.log2(jnp.maximum(largest, 1e-30) * (1.0 / 32700.0)))


def coded(values):
    return jnp.round(values).astype(jnp.int32).astype(I16)


def plain(codes):
    return codes.astype(jnp.int32).astype(F32)


def product_kernel(count_ref, system_ref, feats_ref, grads_ref, out_ref, low_acc, high_acc):
    step = pl.program_id(0)
    steps = pl.num_programs(0)
    rows = feats_ref.shape[0]
    owners = out_ref.shape[0]
    half = low_acc.shape[0] // owners
    blocks = low_acc.shape[1] // LANES
    count = count_ref[0, 0]
    first = system_ref[0, 0]

    def halve(_, span):
        lo, hi = span
        mid = (lo + hi) // 2
        same = system_ref[0, jnp.minimum(mid, count - 1)] == first
        inside = lo < hi
        return (
            jnp.where(inside & same, mid + 1, lo),
            jnp.where(inside & jnp.logical_not(same), mid, hi),
        )

    split, _ = lax.fori_loop(0, 12, halve, (jnp.int32(0), count))
    has_upper = split < count
    base = step * rows
    row = base + lax.broadcasted_iota(jnp.int32, (rows, 1), 0)

    def product(begin, end):
        kept = jnp.where((row >= begin) & (row < end), grads_ref[...].astype(F32), 0.0)
        return lax.dot_general(
            feats_ref[...],
            kept.astype(BF16),
            (((0,), (0,)), ((), ())),
            preferred_element_type=F32,
        )

    @pl.when(step == 0)
    def _():
        low_acc[...] = product(0, split)

    @pl.when((step > 0) & (base < split))
    def _():
        low_acc[...] += product(0, split)

    @pl.when(has_upper & (step == 0))
    def _():
        high_acc[...] = jnp.zeros_like(high_acc)

    @pl.when(has_upper & (base + rows > split) & (base < count))
    def _():
        high_acc[...] += product(split, count)

    def hand_out(low_e, high_e):
        row = lax.broadcasted_iota(jnp.int32, (NOTE, LANES), 0)
        note = jnp.where(row == 0, first.astype(F32), jnp.where(row == 1, low_e, high_e))
        note = coded(note)
        low_by = jnp.exp2(-low_e)
        high_by = None if isinstance(high_e, float) else jnp.exp2(-high_e)
        for owner in range(owners):
            at = slice(owner * half, (owner + 1) * half)
            for block in range(blocks):
                lanes = slice(block * LANES, (block + 1) * LANES)
                low = low_acc[at, lanes] * low_by
                high = jnp.zeros_like(low) if high_by is None else high_acc[at, lanes] * high_by
                to = slice(block * 2 * half, (block + 1) * 2 * half)
                out_ref[owner, to, :] = coded(jnp.concatenate([low, high], axis=0))
            out_ref[owner, blocks * 2 * half :, :] = note

    def largest(ref):
        return jnp.max(jnp.abs(ref[...]), axis=(0, 1), keepdims=True)

    @pl.when((step == steps - 1) & has_upper)
    def _():
        hand_out(exponent(largest(low_acc)), exponent(largest(high_acc)))

    @pl.when((step == steps - 1) & jnp.logical_not(has_upper))
    def _():
        hand_out(exponent(largest(low_acc)), 0.0)


def products(count, system, feats, grads, owners):
    rows, din = feats.shape
    dout = grads.shape[1]
    block = 512
    per_owner = 2 * din // owners * (dout // LANES) + NOTE
    return pl.pallas_call(
        product_kernel,
        grid=(rows // block,),
        in_specs=[
            pl.BlockSpec(memory_space=pltpu.SMEM),
            pl.BlockSpec(memory_space=pltpu.SMEM),
            pl.BlockSpec((block, din), lambda k: (k, 0)),
            pl.BlockSpec((block, dout), lambda k: (k, 0)),
        ],
        out_specs=pl.BlockSpec((owners, per_owner, LANES), lambda k: (0, 0, 0)),
        out_shape=jax.ShapeDtypeStruct((owners, per_owner, LANES), I16),
        scratch_shapes=[pltpu.VMEM((din, dout), F32), pltpu.VMEM((din, dout), F32)],
        compiler_params=pltpu.CompilerParams(vmem_limit_bytes=62 * MIB),
        cost_estimate=pl.CostEstimate(
            flops=2 * rows * din * dout,
            bytes_accessed=2 * rows * (din + dout) + 4 * din * dout,
            transcendentals=0,
        ),
        name="products",
    )(count, system, feats, grads)


def collect_kernel(parts_ref, out_ref, total):
    step = pl.program_id(0)
    nsys, half, dout = total.shape
    blocks = dout // LANES

    @pl.when(step == 0)
    def _():
        total[...] = jnp.zeros_like(total)

    for source in range(parts_ref.shape[0]):
        note = plain(parts_ref[source, blocks * 2 * half :, :])
        low = jnp.max(note[0:1]).astype(jnp.int32)
        high = jnp.minimum(low + 1, nsys - 1)
        low_by, high_by = jnp.exp2(note[1:2]), jnp.exp2(note[2:3])
        for block in range(blocks):
            lanes = slice(block * LANES, (block + 1) * LANES)
            part = plain(parts_ref[source, block * 2 * half : (block + 1) * 2 * half, :])
            total[low, :, lanes] += part[:half] * low_by
            total[high, :, lanes] += part[half:] * high_by

    @pl.when(step == pl.num_programs(0) - 1)
    def _():
        row = lax.broadcasted_iota(jnp.int32, (NOTE, LANES), 0)
        note = jnp.zeros((NOTE, LANES), F32)
        scaled = []
        for system in range(nsys):
            values = total[system]
            e = exponent(jnp.max(jnp.abs(values), axis=(0, 1), keepdims=True))
            note = jnp.where(row == system, e, note)
            scaled.append(values * jnp.exp2(-e))
        rows = nsys * half
        for block in range(blocks):
            lanes = slice(block * LANES, (block + 1) * LANES)
            values = jnp.concatenate([part[:, lanes] for part in scaled], axis=0)
            out_ref[block * rows : (block + 1) * rows, :] = coded(values)
        out_ref[blocks * rows :, :] = coded(note)


def collect(parts, nsys, half, dout):
    sources = parts.shape[0]
    block = 8
    out = (nsys * half * (dout // LANES) + NOTE, LANES)
    return pl.pallas_call(
        collect_kernel,
        grid=(sources // block,),
        in_specs=[pl.BlockSpec((block,) + parts.shape[1:], lambda k: (k, 0, 0))],
        out_specs=pl.BlockSpec(out, lambda k: (0, 0)),
        out_shape=jax.ShapeDtypeStruct(out, I16),
        scratch_shapes=[pltpu.VMEM((nsys, half, dout), F32)],
        compiler_params=pltpu.CompilerParams(vmem_limit_bytes=12 * MIB),
        cost_estimate=pl.CostEstimate(
            flops=2 * parts.size, bytes_accessed=2 * parts.size, transcendentals=0
        ),
        name="collect",
    )(parts)


def hold_kernel(*refs):
    states, held_ref, sems = refs[:-2], refs[-2], refs[-1]
    copies = [
        pltpu.make_async_copy(ref, held_ref.at[k], sems.at[k]) for k, ref in enumerate(states)
    ]
    for copy in copies:
        copy.start()
    for copy in copies:
        copy.wait()


def hold(states):
    shape = (len(states),) + states[0].shape
    return pl.pallas_call(
        hold_kernel,
        in_specs=[pl.BlockSpec(memory_space=pl.ANY)] * len(states),
        out_specs=pl.BlockSpec(memory_space=pltpu.VMEM),
        out_shape=pltpu.VMEM(shape, F32),
        scratch_shapes=[pltpu.SemaphoreType.DMA((len(states),))],
        compiler_params=pltpu.CompilerParams(vmem_limit_bytes=4 * MIB),
        name="hold",
    )(*states)


def unpack(sums, system_sums):
    nsys = system_sums.shape[0] // len(sums)
    rows, lanes = system_sums.shape[1:]
    per_block = nsys * rows
    for rep, ref in enumerate(sums):
        by = jnp.exp2(plain(ref[lanes // LANES * per_block :, :]))
        for block in range(lanes // LANES):
            to = slice(block * LANES, (block + 1) * LANES)
            values = plain(ref[block * per_block : (block + 1) * per_block, :])
            for system in range(nsys):
                system_sums[rep * nsys + system, :, to] = (
                    values[system * rows : (system + 1) * rows] * by[system : system + 1]
                )


def mixed(mix_ref, right):
    n = mix_ref.shape[0] // 2
    near = right.astype(BF16)
    rest = (right - near.astype(F32)).astype(BF16)
    both = jnp.dot(mix_ref[...], near, preferred_element_type=F32)
    more = jnp.dot(mix_ref[:n, :], rest, preferred_element_type=F32)
    return both[:n] + (both[n:] + more)


def begin_kernel(mix_ref, *refs):
    sums, out_ref, system_sums = refs[:-2], refs[-2], refs[-1]
    _, rows, lanes = out_ref.shape
    unpack(sums, system_sums)
    for row in range(0, rows, 8):
        right = system_sums[:, row : row + 8, :].reshape(-1, lanes)
        out_ref[:, row : row + 8, :] = mixed(mix_ref, right).reshape(-1, 8, lanes)


def begin(mix, sums, nsys, rows, dout):
    vmem = pl.BlockSpec(memory_space=pltpu.VMEM)
    return pl.pallas_call(
        begin_kernel,
        in_specs=[vmem] * (1 + len(sums)),
        out_specs=vmem,
        out_shape=pltpu.VMEM((mix.shape[0] // 16, rows, dout), F32),
        scratch_shapes=[pltpu.VMEM((len(sums) * nsys, rows, dout), F32)],
        compiler_params=pltpu.CompilerParams(vmem_limit_bytes=14 * MIB),
        name="begin",
    )(mix, *sums)


def update_kernel(mix_ref, merge_ref, *refs):
    *sums, states, begun = refs[:-6]
    out_weights, out_first, out_second, out_merged, system_sums, merged = refs[-6:]
    step = pl.program_id(0)
    mine, group, lanes = out_weights.shape
    nsys, rows, _ = merged.shape
    reps = states.shape[0]
    n = group * mine * reps
    at = pl.ds(pl.multiple_of(step * group, group), group)
    m = group * nsys
    corr_first = 1.0 - 0.9**10
    corr_second = 1.0 - 0.999**10

    @pl.when(step == 0)
    def _():
        unpack(sums, system_sums)

    def of_experts(kind):
        return states[:, kind * mine : (kind + 1) * mine, at, :].reshape(-1, group, lanes)

    right = system_sums[:, at, :].reshape(-1, lanes)
    grad = begun[:, at, :] + mixed(mix_ref, right).reshape(-1, group, lanes)
    new_first = 0.9 * of_experts(1) + 0.1 * grad
    new_second = 0.999 * of_experts(2) + 0.001 * grad * grad
    scaled = new_second * (1.0 / corr_second)
    below = scaled * lax.rsqrt(scaled) + 1e-08
    inverse = pl.reciprocal(below, approx=True)
    inverse = inverse * (2.0 - below * inverse)
    new_weights = of_experts(0) - new_first * (0.01 / corr_first) * inverse
    out_weights[...] = new_weights[:mine]
    out_first[...] = new_first[:mine]
    out_second[...] = new_second[:mine]
    rounded = new_weights.reshape(n, lanes).astype(BF16)
    both = jnp.dot(merge_ref[...], rounded, preferred_element_type=F32)
    merged[:, at, :] = (both[:m] + both[m:]).reshape(nsys, group, lanes)

    @pl.when(step == pl.num_programs(0) - 1)
    def _():
        out_merged[...] = merged[...].astype(BF16)


def update(mix, merge, sums, states, begun, nsys):
    reps, mine, rows, dout = states.shape
    mine = mine // 3
    group = 8
    whole = lambda g: (0, 0)
    some = lambda g: (0, g, 0)
    return pl.pallas_call(
        update_kernel,
        grid=(rows // group,),
        in_specs=[pl.BlockSpec(a.shape, whole) for a in [mix, merge] + sums]
        + [pl.BlockSpec(memory_space=pltpu.VMEM)] * 2,
        out_specs=[pl.BlockSpec((mine, group, dout), some)] * 3
        + [pl.BlockSpec((nsys, rows, dout), lambda g: (0, 0, 0))],
        out_shape=[jax.ShapeDtypeStruct((mine, rows, dout), F32)] * 3
        + [jax.ShapeDtypeStruct((nsys, rows, dout), BF16)],
        scratch_shapes=[
            pltpu.VMEM((len(sums) * nsys, rows, dout), F32),
            pltpu.VMEM((nsys, rows, dout), F32),
        ],
        compiler_params=pltpu.CompilerParams(vmem_limit_bytes=32 * MIB),
        name="update",
    )(mix, merge, *sums, states, begun)


def prepare_kernel(rep_ref, *refs):
    coefs, (first_ref, mix_ref, merge_ref) = refs[:-3], refs[-3:]
    reps, chips = len(coefs), len(coefs) // 2
    padded, experts = coefs[0].shape
    rows = mix_ref.shape[0] // 2
    begun = first_ref.shape[1]
    columns = begun + mix_ref.shape[1]
    out_rows = merge_ref.shape[0] // 2
    nsys = out_rows // 8
    mine = experts // reps
    chip, core = rep_ref[0] // 2, rep_ref[0] % 2

    def count(shape, axis):
        return lax.broadcasted_iota(jnp.int32, shape, axis)

    expert = count((rows, experts), 0) >> 3
    block = expert // mine
    owner = ((chip + block % chips) % chips) * 2 + (core + block // chips) % 2
    at_expert = owner * mine + expert % mine == count((rows, experts), 1)
    at_expert = at_expert.astype(F32).astype(BF16)
    row = count((padded * reps, columns), 0)
    place = row % padded
    at_system = (count((padded * reps, columns), 1) >> 3) == nsys * (row // padded) + place
    at_system = (at_system & (place < nsys)).astype(F32).astype(BF16)
    at_out = (count((out_rows, padded), 0) >> 3) == count((out_rows, padded), 1)
    at_out = at_out.astype(F32).astype(BF16)
    same_mix = (count((rows, columns), 0) & 7) == (count((rows, columns), 1) & 7)
    same_merge = (count((out_rows, rows), 0) & 7) == (count((out_rows, rows), 1) & 7)
    values = jnp.concatenate([ref[...] for ref in coefs], axis=0)
    near = values.astype(BF16)
    rest = (values - near.astype(F32)).astype(BF16)
    transposed = (((1,), (1,)), ((), ()))
    for k, part in enumerate((near, rest)):
        wide = lax.dot_general(at_expert, part, transposed, preferred_element_type=F32)
        wide = jnp.dot(wide.astype(BF16), at_system, preferred_element_type=F32)
        wide = jnp.where(same_mix, wide, 0.0)
        first_ref[k * rows : (k + 1) * rows, :] = wide[:, :begun].astype(BF16)
        mix_ref[k * rows : (k + 1) * rows, :] = wide[:, begun:].astype(BF16)
        own = jnp.dot(at_out, part[:padded], preferred_element_type=F32)
        own = lax.dot_general(own.astype(BF16), at_expert, transposed, preferred_element_type=F32)
        merge_ref[k * out_rows : (k + 1) * out_rows, :] = jnp.where(same_merge, own, 0.0).astype(BF16)


def prepare(rep, coefs, nsys, begun):
    reps, experts = len(coefs), coefs[0].shape[1]
    vmem = pl.BlockSpec(memory_space=pltpu.VMEM)
    return pl.pallas_call(
        prepare_kernel,
        in_specs=[pl.BlockSpec(memory_space=pltpu.SMEM)] + [vmem] * reps,
        out_specs=[vmem] * 3,
        out_shape=[
            jax.ShapeDtypeStruct((2 * 8 * experts, 8 * begun * nsys), BF16),
            jax.ShapeDtypeStruct((2 * 8 * experts, 8 * (reps - begun) * nsys), BF16),
            jax.ShapeDtypeStruct((2 * 8 * nsys, 8 * experts), BF16),
        ],
        compiler_params=pltpu.CompilerParams(vmem_limit_bytes=12 * MIB),
        name="prepare",
    )(rep, *coefs)


def everywhere(value, axis, moves):
    return [lax.ppermute(value, axis, pairs) for pairs in moves]


def on_device(
    edge_feats, edge_grads, edge_system, edge_count, coef, weights, first_moment, second_moment
):
    owners = lax.axis_size("run")
    reps = lax.axis_size("rep")
    nsys = coef.shape[1]

    chips = reps // 2
    along_x = [
        [((x + dx) % chips * 2 + c, x * 2 + c) for x in range(chips) for c in range(2)]
        for dx in range(1, chips)
    ]
    swap = [(i, i ^ 1) for i in range(reps)]

    def all_reps(value):
        near = [value] + everywhere(value, "rep", along_x)
        return near + [lax.ppermute(part, "rep", swap) for part in near]

    coefs = all_reps(jnp.pad(coef[0], ((0, -nsys % 8), (0, 0))))
    early = [0, chips, chips - 1]
    late = [k for k in range(reps) if k not in early]
    in_turn = [coefs[k] for k in early + late]
    first_mix, mix, merge = prepare(lax.axis_index("rep").reshape(1), in_turn, nsys, len(early))
    first_mix, mix, merge, *state_parts = lax.optimization_barrier(
        (first_mix, mix, merge, weights, first_moment, second_moment)
    )
    states = all_reps(jnp.concatenate(state_parts, axis=0))

    parts = products(edge_count, edge_system, edge_feats[0], edge_grads[0], owners)
    received = lax.all_to_all(parts, "run", 0, 0, tiled=True)
    sums = collect(received, nsys, weights.shape[1], weights.shape[2])
    near = [sums] + everywhere(sums, "rep", along_x)
    *states, after = lax.optimization_barrier((*states, sums))
    swapped = [lax.ppermute(sums, "rep", swap)] + [None] * (chips - 1)
    states, last = lax.optimization_barrier((hold(states), near[chips - 1]))
    swapped[chips - 1] = lax.ppermute(last, "rep", swap)
    begun = begin(first_mix, [sums, swapped[0], last], nsys, *weights.shape[1:])
    begun, near[chips - 2] = lax.optimization_barrier((begun, near[chips - 2]))
    for k in range(chips - 2, 0, -1):
        swapped[k] = lax.ppermute(near[k], "rep", swap)
    sums = near + swapped
    new_weights, new_first, new_second, merged = update(
        mix, merge, [sums[k] for k in late], states, begun, nsys
    )
    return (new_weights, new_first, new_second, merged[None])


def solution(mesh):
    placed = (
        P("rep", "run", None),
        P("rep", "run", None),
        P("rep", "run"),
        P("rep", "run"),
        P("rep", None, None),
        P("rep", "run", None),
        P("rep", "run", None),
        P("rep", "run", None),
    )
    return jax.shard_map(
        on_device,
        mesh=mesh,
        in_specs=placed,
        out_specs=(
            P("rep", "run", None),
            P("rep", "run", None),
            P("rep", "run", None),
            P("rep", None, "run", None),
        ),
        check_vma=False,
    )
```

```python
import jax
import jax.numpy as jnp
from jax import lax
from jax.experimental import pallas as pl
from jax.experimental.pallas import tpu as pltpu
from jax.sharding import PartitionSpec as P

F32 = jnp.float32
BF16 = jnp.bfloat16
I16 = jnp.int16
MIB = 1 << 20
LANES = 128
NOTE = 16


def exponent(largest):
    return jnp.ceil(jnp.log2(jnp.maximum(largest, 1e-30) * (1.0 / 32700.0)))


def coded(values):
    return jnp.round(values).astype(jnp.int32).astype(I16)


def plain(codes):
    return codes.astype(jnp.int32).astype(F32)


def product_kernel(count_ref, system_ref, feats_ref, grads_ref, out_ref, low_acc, high_acc):
    step = pl.program_id(0)
    steps = pl.num_programs(0)
    rows = feats_ref.shape[0]
    owners = out_ref.shape[0]
    half = low_acc.shape[0] // owners
    blocks = low_acc.shape[1] // LANES
    count = count_ref[0, 0]
    first = system_ref[0, 0]

    def halve(_, span):
        lo, hi = span
        mid = (lo + hi) // 2
        same = system_ref[0, jnp.minimum(mid, count - 1)] == first
        inside = lo < hi
        return (
            jnp.where(inside & same, mid + 1, lo),
            jnp.where(inside & jnp.logical_not(same), mid, hi),
        )

    split, _ = lax.fori_loop(0, 12, halve, (jnp.int32(0), count))
    has_upper = split < count
    base = step * rows
    row = base + lax.broadcasted_iota(jnp.int32, (rows, 1), 0)

    def product(begin, end):
        kept = jnp.where((row >= begin) & (row < end), grads_ref[...].astype(F32), 0.0)
        return lax.dot_general(
            feats_ref[...],
            kept.astype(BF16),
            (((0,), (0,)), ((), ())),
            preferred_element_type=F32,
        )

    @pl.when(step == 0)
    def _():
        low_acc[...] = product(0, split)

    @pl.when((step > 0) & (base < split))
    def _():
        low_acc[...] += product(0, split)

    @pl.when(has_upper & (step == 0))
    def _():
        high_acc[...] = jnp.zeros_like(high_acc)

    @pl.when(has_upper & (base + rows > split) & (base < count))
    def _():
        high_acc[...] += product(split, count)

    def hand_out(low_e, high_e):
        row = lax.broadcasted_iota(jnp.int32, (NOTE, LANES), 0)
        note = jnp.where(row == 0, first.astype(F32), jnp.where(row == 1, low_e, high_e))
        note = coded(note)
        low_by = jnp.exp2(-low_e)
        high_by = None if isinstance(high_e, float) else jnp.exp2(-high_e)
        for owner in range(owners):
            at = slice(owner * half, (owner + 1) * half)
            for block in range(blocks):
                lanes = slice(block * LANES, (block + 1) * LANES)
                low = low_acc[at, lanes] * low_by
                high = jnp.zeros_like(low) if high_by is None else high_acc[at, lanes] * high_by
                to = slice(block * 2 * half, (block + 1) * 2 * half)
                out_ref[owner, to, :] = coded(jnp.concatenate([low, high], axis=0))
            out_ref[owner, blocks * 2 * half :, :] = note

    def largest(ref):
        return jnp.max(jnp.abs(ref[...]), axis=(0, 1), keepdims=True)

    @pl.when((step == steps - 1) & has_upper)
    def _():
        hand_out(exponent(largest(low_acc)), exponent(largest(high_acc)))

    @pl.when((step == steps - 1) & jnp.logical_not(has_upper))
    def _():
        hand_out(exponent(largest(low_acc)), 0.0)


def products(count, system, feats, grads, owners):
    rows, din = feats.shape
    dout = grads.shape[1]
    block = 512
    per_owner = 2 * din // owners * (dout // LANES) + NOTE
    return pl.pallas_call(
        product_kernel,
        grid=(rows // block,),
        in_specs=[
            pl.BlockSpec(memory_space=pltpu.SMEM),
            pl.BlockSpec(memory_space=pltpu.SMEM),
            pl.BlockSpec((block, din), lambda k: (k, 0)),
            pl.BlockSpec((block, dout), lambda k: (k, 0)),
        ],
        out_specs=pl.BlockSpec((owners, per_owner, LANES), lambda k: (0, 0, 0)),
        out_shape=jax.ShapeDtypeStruct((owners, per_owner, LANES), I16),
        scratch_shapes=[pltpu.VMEM((din, dout), F32), pltpu.VMEM((din, dout), F32)],
        compiler_params=pltpu.CompilerParams(vmem_limit_bytes=62 * MIB),
        cost_estimate=pl.CostEstimate(
            flops=2 * rows * din * dout,
            bytes_accessed=2 * rows * (din + dout) + 4 * din * dout,
            transcendentals=0,
        ),
        name="products",
    )(count, system, feats, grads)


def collect_kernel(parts_ref, out_ref, total):
    step = pl.program_id(0)
    nsys, half, dout = total.shape
    blocks = dout // LANES

    @pl.when(step == 0)
    def _():
        total[...] = jnp.zeros_like(total)

    for source in range(parts_ref.shape[0]):
        note = plain(parts_ref[source, blocks * 2 * half :, :])
        low = jnp.max(note[0:1]).astype(jnp.int32)
        high = jnp.minimum(low + 1, nsys - 1)
        low_by, high_by = jnp.exp2(note[1:2]), jnp.exp2(note[2:3])
        for block in range(blocks):
            lanes = slice(block * LANES, (block + 1) * LANES)
            part = plain(parts_ref[source, block * 2 * half : (block + 1) * 2 * half, :])
            total[low, :, lanes] += part[:half] * low_by
            total[high, :, lanes] += part[half:] * high_by

    @pl.when(step == pl.num_programs(0) - 1)
    def _():
        row = lax.broadcasted_iota(jnp.int32, (NOTE, LANES), 0)
        note = jnp.zeros((NOTE, LANES), F32)
        scaled = []
        for system in range(nsys):
            values = total[system]
            e = exponent(jnp.max(jnp.abs(values), axis=(0, 1), keepdims=True))
            note = jnp.where(row == system, e, note)
            scaled.append(values * jnp.exp2(-e))
        rows = nsys * half
        for block in range(blocks):
            lanes = slice(block * LANES, (block + 1) * LANES)
            values = jnp.concatenate([part[:, lanes] for part in scaled], axis=0)
            out_ref[block * rows : (block + 1) * rows, :] = coded(values)
        out_ref[blocks * rows :, :] = coded(note)


def collect(parts, nsys, half, dout):
    sources = parts.shape[0]
    block = 8
    out = (nsys * half * (dout // LANES) + NOTE, LANES)
    return pl.pallas_call(
        collect_kernel,
        grid=(sources // block,),
        in_specs=[pl.BlockSpec((block,) + parts.shape[1:], lambda k: (k, 0, 0))],
        out_specs=pl.BlockSpec(out, lambda k: (0, 0)),
        out_shape=jax.ShapeDtypeStruct(out, I16),
        scratch_shapes=[pltpu.VMEM((nsys, half, dout), F32)],
        compiler_params=pltpu.CompilerParams(vmem_limit_bytes=12 * MIB),
        cost_estimate=pl.CostEstimate(
            flops=2 * parts.size, bytes_accessed=2 * parts.size, transcendentals=0
        ),
        name="collect",
    )(parts)


def hold_kernel(*refs):
    states, held_ref, sems = refs[:-2], refs[-2], refs[-1]
    copies = [
        pltpu.make_async_copy(ref, held_ref.at[k], sems.at[k]) for k, ref in enumerate(states)
    ]
    for copy in copies:
        copy.start()
    for copy in copies:
        copy.wait()


def hold(states):
    shape = (len(states),) + states[0].shape
    return pl.pallas_call(
        hold_kernel,
        in_specs=[pl.BlockSpec(memory_space=pl.ANY)] * len(states),
        out_specs=pl.BlockSpec(memory_space=pltpu.VMEM),
        out_shape=pltpu.VMEM(shape, F32),
        scratch_shapes=[pltpu.SemaphoreType.DMA((len(states),))],
        compiler_params=pltpu.CompilerParams(vmem_limit_bytes=4 * MIB),
        name="hold",
    )(*states)


def unpack(sums, system_sums):
    nsys = system_sums.shape[0] // len(sums)
    rows, lanes = system_sums.shape[1:]
    per_block = nsys * rows
    for rep, ref in enumerate(sums):
        by = jnp.exp2(plain(ref[lanes // LANES * per_block :, :]))
        for block in range(lanes // LANES):
            to = slice(block * LANES, (block + 1) * LANES)
            values = plain(ref[block * per_block : (block + 1) * per_block, :])
            for system in range(nsys):
                system_sums[rep * nsys + system, :, to] = (
                    values[system * rows : (system + 1) * rows] * by[system : system + 1]
                )


def mixed(mix_ref, right):
    n = mix_ref.shape[0] // 2
    near = right.astype(BF16)
    rest = (right - near.astype(F32)).astype(BF16)
    both = jnp.dot(mix_ref[...], near, preferred_element_type=F32)
    more = jnp.dot(mix_ref[:n, :], rest, preferred_element_type=F32)
    return both[:n] + (both[n:] + more)


def begin_kernel(mix_ref, *refs):
    sums, out_ref, system_sums = refs[:-2], refs[-2], refs[-1]
    _, rows, lanes = out_ref.shape
    unpack(sums, system_sums)
    for row in range(0, rows, 8):
        right = system_sums[:, row : row + 8, :].reshape(-1, lanes)
        out_ref[:, row : row + 8, :] = mixed(mix_ref, right).reshape(-1, 8, lanes)


def begin(mix, sums, nsys, rows, dout):
    vmem = pl.BlockSpec(memory_space=pltpu.VMEM)
    return pl.pallas_call(
        begin_kernel,
        in_specs=[vmem] * (1 + len(sums)),
        out_specs=vmem,
        out_shape=pltpu.VMEM((mix.shape[0] // 16, rows, dout), F32),
        scratch_shapes=[pltpu.VMEM((len(sums) * nsys, rows, dout), F32)],
        compiler_params=pltpu.CompilerParams(vmem_limit_bytes=14 * MIB),
        name="begin",
    )(mix, *sums)


def update_kernel(mix_ref, merge_ref, *refs):
    *sums, states, begun = refs[:-6]
    out_weights, out_first, out_second, out_merged, system_sums, merged = refs[-6:]
    step = pl.program_id(0)
    mine, group, lanes = out_weights.shape
    nsys, rows, _ = merged.shape
    reps = states.shape[0]
    n = group * mine * reps
    at = pl.ds(pl.multiple_of(step * group, group), group)
    m = group * nsys
    corr_first = 1.0 - 0.9**10
    corr_second = 1.0 - 0.999**10

    @pl.when(step == 0)
    def _():
        unpack(sums, system_sums)

    def of_experts(kind):
        return states[:, kind * mine : (kind + 1) * mine, at, :].reshape(-1, group, lanes)

    right = system_sums[:, at, :].reshape(-1, lanes)
    grad = begun[:, at, :] + mixed(mix_ref, right).reshape(-1, group, lanes)
    new_first = 0.9 * of_experts(1) + 0.1 * grad
    new_second = 0.999 * of_experts(2) + 0.001 * grad * grad
    scaled = new_second * (1.0 / corr_second)
    below = scaled * lax.rsqrt(scaled) + 1e-08
    inverse = pl.reciprocal(below, approx=True)
    inverse = inverse * (2.0 - below * inverse)
    new_weights = of_experts(0) - new_first * (0.01 / corr_first) * inverse
    out_weights[...] = new_weights[:mine]
    out_first[...] = new_first[:mine]
    out_second[...] = new_second[:mine]
    rounded = new_weights.reshape(n, lanes).astype(BF16)
    both = jnp.dot(merge_ref[...], rounded, preferred_element_type=F32)
    merged[:, at, :] = (both[:m] + both[m:]).reshape(nsys, group, lanes)

    @pl.when(step == pl.num_programs(0) - 1)
    def _():
        out_merged[...] = merged[...].astype(BF16)


def update(mix, merge, sums, states, begun, nsys):
    reps, mine, rows, dout = states.shape
    mine = mine // 3
    group = 8
    whole = lambda g: (0, 0)
    some = lambda g: (0, g, 0)
    return pl.pallas_call(
        update_kernel,
        grid=(rows // group,),
        in_specs=[pl.BlockSpec(a.shape, whole) for a in [mix, merge] + sums]
        + [pl.BlockSpec(memory_space=pltpu.VMEM)] * 2,
        out_specs=[pl.BlockSpec((mine, group, dout), some)] * 3
        + [pl.BlockSpec((nsys, rows, dout), lambda g: (0, 0, 0))],
        out_shape=[jax.ShapeDtypeStruct((mine, rows, dout), F32)] * 3
        + [jax.ShapeDtypeStruct((nsys, rows, dout), BF16)],
        scratch_shapes=[
            pltpu.VMEM((len(sums) * nsys, rows, dout), F32),
            pltpu.VMEM((nsys, rows, dout), F32),
        ],
        compiler_params=pltpu.CompilerParams(vmem_limit_bytes=32 * MIB),
        name="update",
    )(mix, merge, *sums, states, begun)


def prepare_kernel(rep_ref, *refs):
    coefs, (first_ref, mix_ref, merge_ref) = refs[:-3], refs[-3:]
    reps, chips = len(coefs), len(coefs) // 2
    padded, experts = coefs[0].shape
    rows = mix_ref.shape[0] // 2
    begun = first_ref.shape[1]
    columns = begun + mix_ref.shape[1]
    out_rows = merge_ref.shape[0] // 2
    nsys = out_rows // 8
    mine = experts // reps
    chip, core = rep_ref[0] // 2, rep_ref[0] % 2

    def count(shape, axis):
        return lax.broadcasted_iota(jnp.int32, shape, axis)

    expert = count((rows, experts), 0) >> 3
    block = expert // mine
    owner = ((chip + block % chips) % chips) * 2 + (core + block // chips) % 2
    at_expert = owner * mine + expert % mine == count((rows, experts), 1)
    at_expert = at_expert.astype(F32).astype(BF16)
    row = count((padded * reps, columns), 0)
    place = row % padded
    at_system = (count((padded * reps, columns), 1) >> 3) == nsys * (row // padded) + place
    at_system = (at_system & (place < nsys)).astype(F32).astype(BF16)
    at_out = (count((out_rows, padded), 0) >> 3) == count((out_rows, padded), 1)
    at_out = at_out.astype(F32).astype(BF16)
    same_mix = (count((rows, columns), 0) & 7) == (count((rows, columns), 1) & 7)
    same_merge = (count((out_rows, rows), 0) & 7) == (count((out_rows, rows), 1) & 7)
    values = jnp.concatenate([ref[...] for ref in coefs], axis=0)
    near = values.astype(BF16)
    rest = (values - near.astype(F32)).astype(BF16)
    transposed = (((1,), (1,)), ((), ()))
    for k, part in enumerate((near, rest)):
        wide = lax.dot_general(at_expert, part, transposed, preferred_element_type=F32)
        wide = jnp.dot(wide.astype(BF16), at_system, preferred_element_type=F32)
        wide = jnp.where(same_mix, wide, 0.0)
        first_ref[k * rows : (k + 1) * rows, :] = wide[:, :begun].astype(BF16)
        mix_ref[k * rows : (k + 1) * rows, :] = wide[:, begun:].astype(BF16)
        own = jnp.dot(at_out, part[:padded], preferred_element_type=F32)
        own = lax.dot_general(own.astype(BF16), at_expert, transposed, preferred_element_type=F32)
        merge_ref[k * out_rows : (k + 1) * out_rows, :] = jnp.where(same_merge, own, 0.0).astype(BF16)


def prepare(rep, coefs, nsys, begun):
    reps, experts = len(coefs), coefs[0].shape[1]
    vmem = pl.BlockSpec(memory_space=pltpu.VMEM)
    return pl.pallas_call(
        prepare_kernel,
        in_specs=[pl.BlockSpec(memory_space=pltpu.SMEM)] + [vmem] * reps,
        out_specs=[vmem] * 3,
        out_shape=[
            jax.ShapeDtypeStruct((2 * 8 * experts, 8 * begun * nsys), BF16),
            jax.ShapeDtypeStruct((2 * 8 * experts, 8 * (reps - begun) * nsys), BF16),
            jax.ShapeDtypeStruct((2 * 8 * nsys, 8 * experts), BF16),
        ],
        compiler_params=pltpu.CompilerParams(vmem_limit_bytes=12 * MIB),
        name="prepare",
    )(rep, *coefs)


def everywhere(value, axis, moves):
    return [lax.ppermute(value, axis, pairs) for pairs in moves]


def on_device(
    edge_feats, edge_grads, edge_system, edge_count, coef, weights, first_moment, second_moment
):
    owners = lax.axis_size("run")
    reps = lax.axis_size("rep")
    nsys = coef.shape[1]

    chips = reps // 2
    along_x = [
        [((x + dx) % chips * 2 + c, x * 2 + c) for x in range(chips) for c in range(2)]
        for dx in range(1, chips)
    ]
    swap = [(i, i ^ 1) for i in range(reps)]

    def all_reps(value):
        near = [value] + everywhere(value, "rep", along_x)
        return near + [lax.ppermute(part, "rep", swap) for part in near]

    coefs = all_reps(jnp.pad(coef[0], ((0, -nsys % 8), (0, 0))))
    early = [0, chips, chips - 1]
    late = [k for k in range(reps) if k not in early]
    in_turn = [coefs[k] for k in early + late]
    first_mix, mix, merge = prepare(lax.axis_index("rep").reshape(1), in_turn, nsys, len(early))
    first_mix, mix, merge, *state_parts = lax.optimization_barrier(
        (first_mix, mix, merge, weights, first_moment, second_moment)
    )
    states = all_reps(jnp.concatenate(state_parts, axis=0))

    parts = products(edge_count, edge_system, edge_feats[0], edge_grads[0], owners)
    received = lax.all_to_all(parts, "run", 0, 0, tiled=True)
    sums = collect(received, nsys, weights.shape[1], weights.shape[2])
    near = [sums] + everywhere(sums, "rep", along_x)
    *states, after = lax.optimization_barrier((*states, sums))
    swapped = [lax.ppermute(sums, "rep", swap)] + [None] * (chips - 1)
    states, last = lax.optimization_barrier((hold(states), near[chips - 1]))
    swapped[chips - 1] = lax.ppermute(last, "rep", swap)
    begun = begin(first_mix, [sums, swapped[0], last], nsys, *weights.shape[1:])
    for k in range(chips - 2, 0, -1):
        swapped[k] = lax.ppermute(near[k], "rep", swap)
    sums = near + swapped
    new_weights, new_first, new_second, merged = update(
        mix, merge, [sums[k] for k in late], states, begun, nsys
    )
    return (new_weights, new_first, new_second, merged[None])


def solution(mesh):
    placed = (
        P("rep", "run", None),
        P("rep", "run", None),
        P("rep", "run"),
        P("rep", "run"),
        P("rep", None, None),
        P("rep", "run", None),
        P("rep", "run", None),
        P("rep", "run", None),
    )
    return jax.shard_map(
        on_device,
        mesh=mesh,
        in_specs=placed,
        out_specs=(
            P("rep", "run", None),
            P("rep", "run", None),
            P("rep", "run", None),
            P("rep", None, "run", None),
        ),
        check_vma=False,
    )
```
